512 devices in a mesh: src: 16 (over z_hi, x), tile: 32 (over y, z_lo, core).
Axes of the slice: x: 4, y: 4, z: 16 (z_hi: 4, z_lo: 4; z = z_hi * 4 + z_lo), core: 2. Of those that a mesh axis runs over, the one named last changes fastest.
Arguments:
- rhs: bfloat16 [4, 1024, 4096], P(None, 'tile', 'src'), may hold values from -6 to 6
- lower_blocks: bfloat16 [6, 1024, 1024], P(None, 'tile'), may hold values from -0.0625 to 0.0625
- dinv: bfloat16 [4, 1024, 1024], P(None, 'tile'), as said below
- adjoint_field: bfloat16 [4096, 4096], P('tile', 'src'), may hold values from -6 to 6
- side_field: bfloat16 [2, 4096, 4096], P(None, 'tile', 'src'), may hold values from -6 to 6
- stencil_coef: float32 [27, 4096], replicated, may hold values from -2 to 2
- cell_row: int32 [4096], replicated, may hold values from 0 to 4095, each once
Outputs:
- wavefield: bfloat16 [4, 1024, 4096], P(None, 'tile', 'src')
- gradient: float32 [4096], P('tile')
The draws below stay inside these ranges and needn't reach their ends.
Inputs may be any that keep to these rules, and one draw needn't show every extreme that they name: Each block of dinv is lower triangular with a diagonal between 0.6 and 1.6.
All inputs are finite; a program needn't handle non-finite values.
Results may differ from the reference program's by a relative error of at most 0.025.
Values may be sent and summed in bfloat16 or wider, within the bound.
A program may use at most 64 MiB of HBM per device.

```python
import math
import jax
import jax.numpy as jnp
from jax import lax

PW = 1024
NP = 4
GY = 64
GZ = 64
F = 4096
NB = 6
NSRC = 4096
N_TILE = 32


def draw_dinv(key, part):
    key = jax.random.fold_in(key, 11)
    first_key, second_key = jax.random.split(key)
    rows = jnp.arange(PW)[:, None]
    cols = jnp.arange(PW)[None, :]
    below = jnp.clip(jax.random.normal(first_key, (NP, PW, PW), jnp.float32), -5.0, 5.0) * (0.8 / math.sqrt(PW))
    middle = jax.random.uniform(second_key, (NP, PW, PW), jnp.float32, 0.8, 1.25)
    values = jnp.where(cols < rows, below, jnp.where(cols == rows, middle, 0.0))
    return values.astype(jnp.bfloat16)


def block_scale(rng, dims, shards, low, top_value):
    level, own = 1.0, jax.random.fold_in(rng, 6)
    for position, parts in shards:
        draws = jnp.exp(jax.random.uniform(jax.random.fold_in(own, position), (parts,), jnp.float32, low / len(shards), top_value / len(shards)))
        level = level * jnp.repeat(draws, dims[position] // parts).reshape([-1 if axis == position else 1 for axis in range(len(dims))])
    return level


def scatter_about(stream_key, shape, deviation, bound, pieces=(), kind=jnp.bfloat16):
    gain = block_scale(stream_key, shape, pieces, -0.22, 0.18) if pieces else 1.0
    drawn = jax.random.normal(stream_key, shape, jnp.float32) * deviation * gain
    return jnp.minimum(jnp.maximum(drawn, -bound), bound).astype(kind)


def setup_inputs(seed: int = 0) -> dict:
    keys = jax.random.split(jax.random.key(seed), 8)
    return {
        "rhs": scatter_about(keys[0], (NP, PW, NSRC), 1.0, 6.0, ((1, 32), (2, 16))),
        "lower_blocks": scatter_about(keys[1], (NB, PW, PW), (2 * F) ** -0.5, 0.0625, ((1, 32),)),
        "dinv": draw_dinv(jax.random.fold_in(keys[7], 71), 0),
        "adjoint_field": scatter_about(keys[3], (F, NSRC), 1.0, 6.0, ((0, 32), (1, 16))),
        "side_field": scatter_about(keys[4], (2, F, NSRC), 1.0, 6.0, ((1, 32), (2, 16))),
        "stencil_coef": scatter_about(keys[5], (27, F), 0.3, 2.0, (), jnp.float32),
        "cell_row": jax.random.permutation(keys[6], F).astype(jnp.int32),
    }


def device_sums(pairs):
    part_rows = PW // N_TILE
    mats = jnp.stack([mat.astype(jnp.float32).reshape(N_TILE, part_rows, PW) for mat, vec in pairs], axis=1)
    vecs = jnp.stack([vec.astype(jnp.float32).reshape(N_TILE, part_rows, -1) for mat, vec in pairs], axis=1)

    def step(carried, inputs):
        mat_part, vec_part = inputs
        term = jnp.einsum('kpc,kps->cs', mat_part, vec_part)
        rounded = lax.optimization_barrier(term.astype(jnp.bfloat16))
        return (carried + rounded.astype(jnp.float32), None)
    start = jnp.zeros((PW, vecs.shape[-1]), jnp.float32)
    total, unused = lax.scan(step, start, (mats, vecs))
    return total

def reference(rhs, lower_blocks, dinv, adjoint_field, side_field, stencil_coef, cell_row):
    solved = []
    for target in range(NP):
        running = rhs[target].astype(jnp.float32)
        for earlier in range(target):
            running = running - jnp.dot(lower_blocks[target * (target - 1) // 2 + earlier], solved[earlier], preferred_element_type=jnp.float32)
        residual = running.astype(jnp.bfloat16)
        solved.append(jnp.dot(dinv[target], residual, preferred_element_type=jnp.float32).astype(jnp.bfloat16))
    adjoint = [None] * NP
    for target in reversed(range(NP)):
        if target == NP - 1:
            wave = solved[target]
        else:
            pairs = [(lower_blocks[later * (later - 1) // 2 + target], adjoint[later]) for later in range(target + 1, NP)]
            wave = (solved[target].astype(jnp.float32) - device_sums(pairs)).astype(jnp.bfloat16)
        adjoint[target] = device_sums([(dinv[target], wave)]).astype(jnp.bfloat16)
    wavefield = jnp.stack(adjoint)
    flat = wavefield.reshape(F, NSRC)
    ordered = jnp.take(flat, cell_row, axis=0).reshape(GY, GZ, NSRC)
    planes = (side_field[0].reshape(GY, GZ, NSRC), ordered, side_field[1].reshape(GY, GZ, NSRC))
    field = jnp.zeros((GY, GZ, NSRC), jnp.float32)
    for offset_x in (-1, 0, 1):
        padded = jnp.pad(planes[offset_x + 1], ((1, 1), (1, 1), (0, 0)))
        for offset_y in (-1, 0, 1):
            for offset_z in (-1, 0, 1):
                number = (offset_x + 1) * 9 + (offset_y + 1) * 3 + (offset_z + 1)
                near = padded[1 + offset_y:1 + offset_y + GY, 1 + offset_z:1 + offset_z + GZ]
                field = field + stencil_coef[number].reshape(GY, GZ, 1) * near.astype(jnp.float32)
    summed = lax.optimization_barrier(jnp.sum(adjoint_field.astype(jnp.float32) * field.reshape(F, NSRC), axis=1))
    gradient = summed * (1.0 / math.sqrt(NSRC))
    return (wavefield, gradient)
```

```python
import functools

import jax
import jax.numpy as jnp
from jax import lax
from jax.experimental import pallas as pl
from jax.experimental.pallas import tpu as pltpu
from jax.sharding import PartitionSpec as P

MESH = pl.DeviceIdType.MESH
F32 = jnp.float32
BF16 = jnp.bfloat16
NY = 4
NC = 8
PANELS = 4
PART = 32
SRC = 32
QUARTER = 256
PW = 1024
WIDE = 1280
NN = (((1,), (0,)), ((), ()))
NT = (((1,), (1,)), ((), ()))

ORDER = [("d", 0), ("l", 0), ("d", 1), ("l", 1), ("l", 2), ("d", 2), ("l", 3), ("l", 4), ("l", 5), ("d", 3)]
PLACE = {unit: number for number, unit in enumerate(ORDER)}


def block_of(later, earlier):
    return later * (later - 1) // 2 + earlier


def dot(a, b, dims):
    return lax.dot_general(a, b, dims, preferred_element_type=F32)


def kernel(
    rhs, lower, dinv, adj, side, coef, cells,
    wave_out, grad_out,
    dcols, lrows, x_send, x_got, s_send, s_got, halo, order, perm, acc,
    part_send, part_got, y_full, z_own, z_all, grid, field, w_send, w_got,
    g1_send, g1_got, g2_send, g2_got,
    dy_s, dy_r, xa_s, xa_r, sa_s, sa_r, mz_s, mz_r, mc_s, mc_r, st_s, st_r,
    za_s, za_r, ha_s, ha_r, wf_s, wf_r, g1_s, g1_r, g2_s, g2_r,
):
    s = lax.axis_index("src")
    t = lax.axis_index("tile")
    x, zh = lax.rem(s, 4), lax.div(s, 4)
    y, zc = lax.div(t, NC), lax.rem(t, NC)
    zl, core = lax.div(zc, 2), lax.rem(zc, 2)
    z = zh * 4 + zl

    def dev(x, y, z, c):
        return (lax.div(z, 4) * 4 + x, (y * 4 + lax.rem(z, 4)) * 2 + c)

    def y_peer(d):
        return dev(x, lax.rem(y + d, NY), z, core)

    def z_peer(d):
        return dev(x, y, lax.rem(z + d + 16, 16), core)

    def c_index(d):
        return lax.rem(zc + d, NC)

    def c_peer(d):
        return (s, y * NC + c_index(d))

    def s_peer(d):
        return (lax.rem(s + d, 16), t)

    sibling = dev(x, y, z, 1 - core)
    started = []

    def send(src, dst, send_sem, recv_sem, device):
        copy = pltpu.make_async_remote_copy(
            src_ref=src, dst_ref=dst, send_sem=send_sem, recv_sem=recv_sem,
            device_id=device, device_id_type=MESH,
        )
        copy.start()
        started.append(copy)
        return copy

    barrier = pltpu.get_barrier_semaphore()
    peers = [y_peer(d) for d in (1, 2, 3)] + [c_peer(d) for d in range(1, NC)]
    peers += [z_peer(d) for d in (1, -1, 2, -2)] + [s_peer(d) for d in range(1, 16)]
    for peer in peers:
        pl.semaphore_signal(barrier, inc=1, device_id=peer, device_id_type=MESH)

    x_send[...] = rhs[...].astype(F32).reshape(PANELS * PART, 256).T.astype(BF16)
    own_cols = pl.ds(pl.multiple_of(y * QUARTER, QUARTER), QUARTER)
    for j in range(PANELS):
        dcols[j, y, zc] = dinv[j, :, own_cols]
    for b in range(6):
        lrows[b, zc] = lower[b]
    own_rows = pl.ds(pl.multiple_of(zc * SRC, SRC), SRC)
    x_got[zc] = x_send[own_rows, :]
    pl.semaphore_wait(barrier, len(peers))

    dy = []
    for j in range(PANELS):
        row = []
        for d in (1, 2, 3):
            cols = pl.ds(pl.multiple_of(lax.rem(y + d, NY) * QUARTER, QUARTER), QUARTER)
            row.append(send(dinv.at[j, :, cols], dcols.at[j, y, zc], dy_s.at[j, d - 1], dy_r.at[j, d - 1], y_peer(d)))
        dy.append(row)
        if j == 0:
            xa = []
            for d in range(1, NC):
                part = pl.ds(pl.multiple_of(c_index(d) * SRC, SRC), SRC)
                xa.append(send(x_send.at[part, :], x_got.at[zc], xa_s.at[d - 1], xa_r.at[d - 1], c_peer(d)))

    def unit_ref(unit, slot):
        kind, number = unit
        return dcols.at[number, :, slot] if kind == "d" else lrows.at[number, slot]

    def slot_at(d):
        return lax.rem(zl + d, 4) * 2 + core

    mz = {}
    mc = {}

    def push(unit):
        n = PLACE[unit]
        if unit[0] == "d":
            for copy in dy[unit[1]]:
                copy.wait_recv()
        mine = unit_ref(unit, zc)
        far = 2 - 4 * lax.rem(core + n, 2)
        mz[unit] = [
            send(mine, mine, mz_s.at[n, k], mz_r.at[n, k], z_peer(d)) for k, d in enumerate((1, -1, far))
        ]
        mc[unit] = [send(mine, mine, mc_s.at[n, 0], mc_r.at[n, 0], sibling)]

    def pump(unit):
        n = PLACE[unit]
        for k, d in enumerate((3, 1, 2)):
            mz[unit][k].wait_recv()
            here = unit_ref(unit, slot_at(d))
            mc[unit].append(send(here, here, mc_s.at[n, k + 1], mc_r.at[n, k + 1], sibling))

    def ready(unit):
        for copy in mc[unit]:
            copy.wait_recv()

    push(("l", 0))
    for unit in ORDER:
        if unit != ("l", 0):
            push(unit)

    s_send[:, 0:128] = adj[...].astype(F32).T.astype(BF16)
    s_send[:, 128:256] = side[0].astype(F32).T.astype(BF16)
    s_send[:, 256:384] = side[1].astype(F32).T.astype(BF16)
    s_got[zc] = s_send[own_rows, :]
    sa = []
    for d in range(1, NC):
        part = pl.ds(pl.multiple_of(c_index(d) * SRC, SRC), SRC)
        sa.append(send(s_send.at[part, :], s_got.at[zc], sa_s.at[d - 1], sa_r.at[d - 1], c_peer(d)))

    lane = lax.broadcasted_iota(jnp.int32, (SRC, 128), 1)
    for copy in xa:
        copy.wait_recv()
    for p in range(PANELS):
        for half in range(2):
            block = jnp.zeros((SRC, 128), F32)
            for q in range(4):
                piece = pltpu.roll(x_got[half * 4 + q].astype(F32), ((q - p) * PART) % 128, 1)
                block = jnp.where(lane // PART == q, piece, block)
            acc[p, :, half * 128:(half + 1) * 128] = block

    order[0:8, :] = cells[pl.ds(pl.multiple_of(lax.rem(y + 3, NY) * 8, 8), 8), :]
    left = jnp.where(y == 0, -1, order[7:8, :])
    order[8:16, :] = cells[pl.ds(pl.multiple_of(lax.rem(y + 1, NY) * 8, 8), 8), :]
    right = jnp.where(y == NY - 1, -1, order[8:9, :])
    middle = cells[pl.ds(pl.multiple_of(y * 8, 8), 8), :]
    wanted = [left] + [middle[i:i + 1, :] for i in range(8)] + [right]

    def fill(i, carry):
        rows = lax.broadcasted_iota(jnp.int32, (QUARTER, 128), 0) + i * QUARTER
        at = pl.ds(pl.multiple_of(i * QUARTER, QUARTER), QUARTER)
        for n, row in enumerate(wanted):
            hit = jnp.where(rows == row, 1.0, 0.0).astype(BF16)
            perm[at, n * 128:(n + 1) * 128] = hit
        return carry

    lax.fori_loop(0, 16, fill, 0)

    def share(step, value):
        part_send[step] = value.astype(BF16)
        return [
            send(part_send.at[step], part_got.at[step, d - 1], st_s.at[step, d - 1], st_r.at[step, d - 1], y_peer(d))
            for d in (1, 2, 3)
        ]

    def total(step, copies):
        for copy in copies:
            copy.wait_recv()
        value = part_send[step].astype(F32)
        for d in range(3):
            value = value + part_got[step, d].astype(F32)
        return value

    def d_whole(j):
        return dcols[j].reshape(PW, QUARTER)

    def l_whole(later, earlier):
        return lrows[block_of(later, earlier)].reshape(QUARTER, PW)

    pump(("d", 0))
    pump(("l", 0))
    ready(("d", 0))
    windows = {
        0: [("d", 1), ("l", 1)],
        1: [("l", 2), ("d", 2), ("l", 3)],
        2: [("l", 4), ("l", 5), ("d", 3)],
        3: [],
    }
    for j in range(PANELS):
        resid = acc[j].astype(BF16)
        copies = share(j, dot(resid, d_whole(j), NT))
        for unit in windows[j]:
            pump(unit)
        if j + 1 < PANELS:
            for k in range(j):
                ready(("l", block_of(j + 1, k)))
                acc[j + 1] = acc[j + 1] - dot(y_full[k], l_whole(j + 1, k), NT)
            ready(("l", block_of(j + 1, j)))
            ready(("d", j + 1))
        if j == 3:
            for copy in sa:
                copy.wait_recv()
            ha = [
                send(s_got.at[7, :, pl.ds(128, 256)], halo.at[0], ha_s.at[0], ha_r.at[0], y_peer(1)),
                send(s_got.at[0, :, pl.ds(128, 256)], halo.at[1], ha_s.at[1], ha_r.at[1], y_peer(3)),
            ]
        y_full[j] = total(j, copies).astype(BF16)
        if j + 1 < PANELS:
            acc[j + 1] = acc[j + 1] - dot(y_full[j], l_whole(j + 1, j), NT)

    zpos = lax.rem(lax.broadcasted_iota(jnp.int32, (1, PW), 1), 64)
    own_cells = pl.ds(pl.multiple_of(y * PW, PW), PW)

    def stencil(plane, offset_x):
        value = jnp.zeros((SRC, PW), F32)
        for offset_y in (-1, 0, 1):
            for offset_z in (-1, 0, 1):
                number = (offset_x + 1) * 9 + (offset_y + 1) * 3 + (offset_z + 1)
                weight = coef[number:number + 1, own_cells]
                if offset_z == -1:
                    weight = jnp.where(zpos > 0, weight, 0.0)
                if offset_z == 1:
                    weight = jnp.where(zpos < 63, weight, 0.0)
                shift = offset_y * 64 + offset_z
                near = pltpu.roll(plane, (-shift) % WIDE, 1) if shift else plane
                value = value + weight * near[:, 128:128 + PW]
        return value

    def side_plane(n):
        low = 128 * (n + 1)
        first = jnp.where(y == 0, 0.0, halo[0, :, 128 * n:128 * (n + 1)].astype(F32))
        last = jnp.where(y == NY - 1, 0.0, halo[1, :, 128 * n:128 * (n + 1)].astype(F32))
        inner = [s_got[i, :, low:low + 128].astype(F32) for i in range(NC)]
        return jnp.concatenate([first] + inner + [last], axis=1)

    def order_cells(j):
        value = jnp.zeros((SRC, WIDE), F32)
        for q in range(NY):
            rows = slice((j * NY + q) * QUARTER, (j * NY + q + 1) * QUARTER)
            value = value + dot(z_all[j, q], perm[rows, :], NN)
        return value

    za = {}
    later_term = {}
    whole = y_full[3]
    for j in reversed(range(PANELS)):
        z_j = dot(whole, d_whole(j), NN).astype(BF16)
        z_own[j] = z_j
        if j > 0:
            term = dot(z_j, l_whole(j, j - 1), NN)
            if j - 1 in later_term:
                term = term + later_term[j - 1]
            copies = share(7 - j, term)
        z_all[j, y] = z_j
        za[j] = [
            send(z_own.at[j], z_all.at[j, y], za_s.at[j, d - 1], za_r.at[j, d - 1], y_peer(d)) for d in (1, 2, 3)
        ]
        if j > 0:
            for earlier in range(j - 1):
                more = dot(z_j, l_whole(j, earlier), NN)
                later_term[earlier] = later_term[earlier] + more if earlier in later_term else more
            if j == 3:
                for copy in ha:
                    copy.wait_recv()
                field[...] = stencil(side_plane(0), -1) + stencil(side_plane(1), 1)
            else:
                for copy in za[j + 1]:
                    copy.wait_recv()
                grid[...] = order_cells(j + 1) if j == 2 else grid[...] + order_cells(j + 1)
            whole = (y_full[j - 1].astype(F32) - total(7 - j, copies)).astype(BF16)

    for d in range(NC):
        pass
    z_f32 = [z_own[p].astype(F32) for p in range(PANELS)]
    for n in range(NC):
        block = jnp.zeros((SRC, 128), F32)
        for p in range(PANELS):
            piece = z_f32[p][:, (n // 4) * 128:(n // 4 + 1) * 128]
            piece = pltpu.roll(piece, ((p - n % 4) * PART) % 128, 1)
            block = jnp.where(lane // PART == p, piece, block)
        w_send[n] = block.astype(BF16)
    w_got[zc] = w_send[zc]
    wf = []
    for d in range(1, NC):
        wf.append(send(w_send.at[c_index(d)], w_got.at[zc], wf_s.at[d - 1], wf_r.at[d - 1], c_peer(d)))

    for copy in za[1]:
        copy.wait_recv()
    grid[...] = grid[...] + order_cells(1)
    for copy in za[0]:
        copy.wait_recv()
    field_all = field[...] + stencil(grid[...] + order_cells(0), 0)
    for n in range(NC):
        here = s_got[n, :, 0:128].astype(F32) * field_all[:, n * 128:(n + 1) * 128]
        g1_send[n] = jnp.sum(here, axis=0, keepdims=True)

    g1 = []
    for d in range(1, NC):
        g1.append(send(g1_send.at[c_index(d)], g1_got.at[d - 1], g1_s.at[d - 1], g1_r.at[d - 1], c_peer(d)))
    for copy in g1:
        copy.wait_recv()
    group = g1_send[zc]
    for d in range(1, NC):
        group = group + g1_got[d - 1]
    g2_send[...] = group
    g2 = []
    for d in range(1, 16):
        g2.append(send(g2_send, g2_got.at[d - 1], g2_s.at[d - 1], g2_r.at[d - 1], s_peer(d)))

    for copy in wf:
        copy.wait_recv()
    back = w_got[...].astype(F32).reshape(256, 128).T
    wave_out[...] = back.reshape(PANELS, PART, 256).astype(BF16)

    for copy in g2:
        copy.wait_recv()
    for d in range(1, 16):
        group = group + g2_got[d - 1]
    grad_out[...] = group * (1.0 / 64.0)
    for copy in started:
        copy.wait_send()


def shards(rhs, lower_blocks, dinv, adjoint_field, side_field, stencil_coef, cell_row):
    dma = pltpu.SemaphoreType.DMA
    pairs = [(4, 3), (7,), (7,), (10, 3), (10, 4), (7, 3), (4, 3), (2,), (7,), (7,), (15,)]
    wavefield, gradient = pl.pallas_call(
        kernel,
        out_shape=(
            jax.ShapeDtypeStruct((PANELS, PART, 256), BF16),
            jax.ShapeDtypeStruct((1, 128), F32),
        ),
        in_specs=[pl.BlockSpec(memory_space=pltpu.VMEM)] * 7,
        out_specs=(pl.BlockSpec(memory_space=pltpu.VMEM),) * 2,
        scratch_shapes=[
            pltpu.VMEM((PANELS, NY, NC, PART, QUARTER), BF16),
            pltpu.VMEM((6, NC, PART, PW), BF16),
            pltpu.VMEM((256, 128), BF16),
            pltpu.VMEM((NC, SRC, 128), BF16),
            pltpu.VMEM((256, 384), BF16),
            pltpu.VMEM((NC, SRC, 384), BF16),
            pltpu.VMEM((2, SRC, 256), BF16),
            pltpu.VMEM((16, 128), jnp.int32),
            pltpu.VMEM((4096, WIDE), BF16),
            pltpu.VMEM((PANELS, SRC, QUARTER), F32),
            pltpu.VMEM((7, SRC, PW), BF16),
            pltpu.VMEM((7, 3, SRC, PW), BF16),
            pltpu.VMEM((PANELS, SRC, PW), BF16),
            pltpu.VMEM((PANELS, SRC, QUARTER), BF16),
            pltpu.VMEM((PANELS, NY, SRC, QUARTER), BF16),
            pltpu.VMEM((SRC, WIDE), F32),
            pltpu.VMEM((SRC, PW), F32),
            pltpu.VMEM((NC, SRC, 128), BF16),
            pltpu.VMEM((NC, SRC, 128), BF16),
            pltpu.VMEM((NC, 1, 128), F32),
            pltpu.VMEM((NC - 1, 1, 128), F32),
            pltpu.VMEM((1, 128), F32),
            pltpu.VMEM((15, 1, 128), F32),
        ]
        + [dma(shape) for shape in pairs for _ in range(2)],
        compiler_params=pltpu.CompilerParams(
            collective_id=0, has_side_effects=True, vmem_limit_bytes=48 * 1024 * 1024
        ),
        cost_estimate=pl.CostEstimate(flops=10**9, bytes_accessed=4 * 10**6, transcendentals=0),
    )(rhs, lower_blocks, dinv, adjoint_field, side_field, stencil_coef, cell_row.reshape(32, 128))
    return wavefield, gradient.reshape(128)


def solution(mesh):
    in_specs = (
        P(None, "tile", "src"),
        P(None, "tile", None),
        P(None, "tile", None),
        P("tile", "src"),
        P(None, "tile", "src"),
        P(),
        P(),
    )
    out_specs = (P(None, "tile", "src"), P("tile"))
    return jax.shard_map(shards, mesh=mesh, in_specs=in_specs, out_specs=out_specs, check_vma=False)
```

```python
import functools

import jax
import jax.numpy as jnp
from jax import lax
from jax.experimental import pallas as pl
from jax.experimental.pallas import tpu as pltpu
from jax.sharding import PartitionSpec as P

MESH = pl.DeviceIdType.MESH
F32 = jnp.float32
BF16 = jnp.bfloat16
NY = 4
NC = 8
PANELS = 4
PART = 32
SRC = 32
QUARTER = 256
PW = 1024
WIDE = 1280
NN = (((1,), (0,)), ((), ()))
NT = (((1,), (1,)), ((), ()))

ORDER = [("d", 0), ("l", 0), ("d", 1), ("l", 1), ("l", 2), ("d", 2), ("l", 3), ("l", 4), ("l", 5), ("d", 3)]
QUARTERED = [(), (), (2,), (0, 1, 2), (2,), (0, 1, 2), (2,), (0, 1, 2), (2,), (0, 1, 2)]
PLACE = {unit: number for number, unit in enumerate(ORDER)}


def block_of(later, earlier):
    return later * (later - 1) // 2 + earlier


def dot(a, b, dims):
    return lax.dot_general(a, b, dims, preferred_element_type=F32)


def kernel(
    rhs, lower, dinv, adj, side, coef_all, cells_all,
    wave_out, grad_out,
    rhs_in, adj_in, side_in, coef, cells,
    dcols, lrows, x_send, x_got, s_send, s_got, halo, order, perm, acc,
    part_send, part_got, y_full, z_own, z_all, grid, field, w_send, w_got,
    g1_send, g1_got, g2_send, g2_got,
    in_s, dy_s, dy_r, xa_s, xa_r, sa_s, sa_r, mo_s, mz_r, mq_r, mx_r, mc_r, st_s, st_r,
    za_s, za_r, ha_s, ha_r, wf_s, wf_r, g1_s, g1_r, g2_s, g2_r, tick,
):
    s = lax.axis_index("src")
    t = lax.axis_index("tile")
    x, zh = lax.rem(s, 4), lax.div(s, 4)
    y, zc = lax.div(t, NC), lax.rem(t, NC)
    zl, core = lax.div(zc, 2), lax.rem(zc, 2)
    z = zh * 4 + zl

    def dev(x, y, z, c):
        return (lax.div(z, 4) * 4 + x, (y * 4 + lax.rem(z, 4)) * 2 + c)

    def y_peer(d):
        return dev(x, lax.rem(y + d, NY), z, core)

    def x_peer(d):
        return dev(lax.rem(x + d, 4), y, z, core)

    def z_peer(d):
        return dev(x, y, lax.rem(z + d + 16, 16), core)

    def c_index(d):
        return lax.rem(zc + d, NC)

    def c_peer(d):
        return (s, y * NC + c_index(d))

    def s_peer(d):
        return (lax.rem(s + d, 16), t)

    sibling = dev(x, y, z, 1 - core)

    def send(src, dst, send_sem, recv_sem, device):
        pltpu.make_async_remote_copy(
            src_ref=src, dst_ref=dst, send_sem=send_sem, recv_sem=recv_sem,
            device_id=device, device_id_type=MESH,
        ).start()

    def received(ref, sem):
        pltpu.make_async_remote_copy(
            src_ref=ref, dst_ref=ref, send_sem=sem, recv_sem=sem,
            device_id=sibling, device_id_type=MESH,
        ).wait_recv()

    def sent(ref, sem):
        pltpu.make_async_remote_copy(
            src_ref=ref, dst_ref=ref, send_sem=sem, recv_sem=sem,
            device_id=sibling, device_id_type=MESH,
        ).wait_send()

    def signal(sem, device):
        pl.semaphore_signal(sem, inc=1, device_id=device, device_id_type=MESH)

    barrier = pltpu.get_barrier_semaphore()
    peers = [y_peer(d) for d in (1, 2, 3)] + [c_peer(d) for d in range(1, NC)]
    peers += [z_peer(d) for d in (1, -1, 2, -2)] + [x_peer(d) for d in (1, 2, 3)]
    for peer in peers:
        signal(barrier, peer)

    own_cols = pl.ds(pl.multiple_of(y * QUARTER, QUARTER), QUARTER)
    own_rows = pl.ds(pl.multiple_of(zc * SRC, SRC), SRC)
    own_cells = pl.ds(pl.multiple_of(y * PW, PW), PW)
    loads = [
        pltpu.make_async_copy(rhs, rhs_in, in_s.at[0]),
        pltpu.make_async_copy(dinv.at[:, :, own_cols], dcols.at[:, y, zc], in_s.at[1]),
        pltpu.make_async_copy(lower, lrows.at[:, zc], in_s.at[2]),
        pltpu.make_async_copy(cells_all, cells, in_s.at[3]),
        pltpu.make_async_copy(adj, adj_in, in_s.at[4]),
        pltpu.make_async_copy(side, side_in, in_s.at[5]),
        pltpu.make_async_copy(coef_all.at[:, own_cells], coef, in_s.at[6]),
    ]
    for load in loads:
        load.start()
    loads[0].wait()
    x_send[...] = rhs_in[...].astype(F32).reshape(PANELS * PART, 256).T.astype(BF16)
    x_got[zc] = x_send[own_rows, :]
    loads[1].wait()
    loads[2].wait()
    pl.semaphore_wait(barrier, len(peers))

    def spread(j):
        for d in (1, 2, 3):
            cols = pl.ds(pl.multiple_of(lax.rem(y + d, NY) * QUARTER, QUARTER), QUARTER)
            send(dinv.at[j, :, cols], dcols.at[j, y, zc], dy_s.at[j], dy_r.at[j], y_peer(d))

    spread(0)
    for d in range(1, NC):
        part = pl.ds(pl.multiple_of(c_index(d) * SRC, SRC), SRC)
        send(x_send.at[part, :], x_got.at[zc], xa_s, xa_r, c_peer(d))

    def unit_ref(unit, slot):
        kind, number = unit
        return dcols.at[number, :, slot] if kind == "d" else lrows.at[number, slot]

    def unit_slots(unit, count):
        kind, number = unit
        return dcols.at[number, :, pl.ds(0, count)] if kind == "d" else lrows.at[number, pl.ds(0, count)]

    def quarter_ref(unit, slot):
        kind, number = unit
        if kind == "d":
            return dcols.at[number, x, slot]
        return lrows.at[number, slot, :, pl.ds(pl.multiple_of(x * QUARTER, QUARTER), QUARTER)]

    def quarters(count):
        rows, columns = {1: (1, 1), 2: (1, 2), 3: (3, 1), 6: (3, 2), 9: (3, 3)}[count]
        return dcols.at[0, pl.ds(0, rows), pl.ds(0, columns)]

    def slot_at(d):
        return lax.rem(zl + d, 4) * 2 + core

    from_slots = (3, 1, 2)

    def push(unit):
        n = PLACE[unit]
        if unit[0] == "d":
            received(dcols.at[unit[1], pl.ds(0, 3), 0], dy_r.at[unit[1]])
        far = 2 - 4 * lax.rem(core + n, 2)
        for k, d in enumerate((1, -1, far)):
            if k in QUARTERED[n]:
                ref, sem = quarter_ref(unit, zc), mq_r
            else:
                ref, sem = unit_ref(unit, zc), mz_r
            send(ref, ref, mo_s.at[n], sem.at[n], z_peer(d))
        mine = unit_ref(unit, zc)
        send(mine, mine, mo_s.at[n], mc_r.at[n], sibling)

    def to_sibling(unit, k):
        here = unit_ref(unit, slot_at(from_slots[k]))
        send(here, here, mo_s.at[PLACE[unit]], mc_r.at[PLACE[unit]], sibling)

    def pump(unit):
        n = PLACE[unit]
        if QUARTERED[n]:
            received(quarters(len(QUARTERED[n])), mq_r.at[n])
            for k in QUARTERED[n]:
                here = quarter_ref(unit, slot_at(from_slots[k]))
                for d in (1, 2, 3):
                    send(here, here, mo_s.at[n], mx_r.at[n], x_peer(d))
        direct = [k for k in range(3) if k not in QUARTERED[n]]
        if direct:
            received(unit_slots(unit, len(direct)), mz_r.at[n])
            for k in direct:
                to_sibling(unit, k)

    def finish(unit):
        n = PLACE[unit]
        received(quarters(3 * len(QUARTERED[n])), mx_r.at[n])
        for k in QUARTERED[n]:
            to_sibling(unit, k)

    def ready(unit):
        received(unit_slots(unit, 4), mc_r.at[PLACE[unit]])

    push(("l", 0))
    for j in (1, 2, 3):
        spread(j)
    for unit in ORDER:
        if unit != ("l", 0):
            push(unit)

    for d in (2, -2):
        signal(tick.at[0], z_peer(d))

    loads[4].wait()
    loads[5].wait()
    s_send[:, 0:128] = adj_in[...].astype(F32).T.astype(BF16)
    s_send[:, 128:256] = side_in[0].astype(F32).T.astype(BF16)
    s_send[:, 256:384] = side_in[1].astype(F32).T.astype(BF16)
    s_got[zc] = s_send[own_rows, :]
    for d in range(1, NC):
        part = pl.ds(pl.multiple_of(c_index(d) * SRC, SRC), SRC)
        send(s_send.at[part, :], s_got.at[zc], sa_s, sa_r, c_peer(d))

    loads[3].wait()
    order[0:8, :] = cells[pl.ds(pl.multiple_of(lax.rem(y + 3, NY) * 8, 8), 8), :]
    left = jnp.where(y == 0, -1, order[7:8, :])
    order[8:16, :] = cells[pl.ds(pl.multiple_of(lax.rem(y + 1, NY) * 8, 8), 8), :]
    right = jnp.where(y == NY - 1, -1, order[8:9, :])
    middle = cells[pl.ds(pl.multiple_of(y * 8, 8), 8), :]
    wanted = [left] + [middle[i:i + 1, :] for i in range(8)] + [right]

    def fill(i, carry):
        rows = lax.broadcasted_iota(jnp.int32, (QUARTER, 128), 0) + i * QUARTER
        at = pl.ds(pl.multiple_of(i * QUARTER, QUARTER), QUARTER)
        for n, row in enumerate(wanted):
            hit = jnp.where(rows == row, 1.0, 0.0).astype(BF16)
            perm[at, n * 128:(n + 1) * 128] = hit
        return carry

    lax.fori_loop(0, 16, fill, 0)

    lane = lax.broadcasted_iota(jnp.int32, (SRC, 128), 1)
    received(x_got.at[pl.ds(0, NC - 1)], xa_r)
    for p in range(PANELS):
        for half in range(2):
            block = jnp.zeros((SRC, 128), F32)
            for q in range(4):
                piece = pltpu.roll(x_got[half * 4 + q].astype(F32), ((q - p) * PART) % 128, 1)
                block = jnp.where(lane // PART == q, piece, block)
            acc[p, :, half * 128:(half + 1) * 128] = block

    def share(step, value):
        part_send[step] = value.astype(BF16)
        for d in (1, 2, 3):
            send(part_send.at[step], part_got.at[step, d - 1], st_s.at[step], st_r.at[step], y_peer(d))

    def total(step):
        received(part_got.at[step], st_r.at[step])
        value = part_send[step].astype(F32)
        for d in range(3):
            value = value + part_got[step, d].astype(F32)
        return value

    def d_whole(j):
        return dcols[j].reshape(PW, QUARTER)

    def l_whole(later, earlier):
        return lrows[block_of(later, earlier)].reshape(QUARTER, PW)

    def take(later, earlier):
        acc[later] = acc[later] - dot(y_full[earlier], l_whole(later, earlier), NT)

    pump(("d", 0))
    pump(("l", 0))
    ready(("d", 0))
    for j in range(PANELS):
        share(j, dot(acc[j].astype(BF16), d_whole(j), NT))
        if j == 0:
            pump(("d", 1))
            pump(("l", 1))
            finish(("d", 1))
            pump(("l", 2))
            ready(("l", 0))
            ready(("d", 1))
            pl.semaphore_wait(tick.at[0], 2)
            for d in (4, -4):
                signal(tick.at[1], z_peer(d))
        if j == 1:
            finish(("l", 1))
            finish(("l", 2))
            pump(("d", 2))
            pump(("l", 3))
            ready(("l", 1))
            take(2, 0)
            finish(("d", 2))
            pump(("l", 4))
            ready(("l", 2))
            ready(("d", 2))
            pl.semaphore_wait(tick.at[1], 2)
            for d in (1, 2, 3):
                signal(tick.at[2], x_peer(d))
        if j == 2:
            finish(("l", 3))
            pump(("l", 5))
            finish(("l", 4))
            pump(("d", 3))
            ready(("l", 3))
            take(3, 0)
            ready(("l", 4))
            take(3, 1)
            finish(("l", 5))
            finish(("d", 3))
            ready(("l", 5))
            ready(("d", 3))
        if j == 3:
            pl.semaphore_wait(tick.at[2], 3)
            received(s_got.at[pl.ds(0, NC - 1)], sa_r)
            send(s_got.at[7, :, pl.ds(128, 256)], halo.at[0], ha_s, ha_r, y_peer(1))
            send(s_got.at[0, :, pl.ds(128, 256)], halo.at[1], ha_s, ha_r, y_peer(3))
        y_full[j] = total(j).astype(BF16)
        if j + 1 < PANELS:
            take(j + 1, j)

    loads[6].wait()
    zpos = lax.rem(lax.broadcasted_iota(jnp.int32, (1, PW), 1), 64)

    def stencil(plane, offset_x):
        value = jnp.zeros((SRC, PW), F32)
        for offset_y in (-1, 0, 1):
            for offset_z in (-1, 0, 1):
                number = (offset_x + 1) * 9 + (offset_y + 1) * 3 + (offset_z + 1)
                weight = coef[number:number + 1, :]
                if offset_z == -1:
                    weight = jnp.where(zpos > 0, weight, 0.0)
                if offset_z == 1:
                    weight = jnp.where(zpos < 63, weight, 0.0)
                shift = offset_y * 64 + offset_z
                near = pltpu.roll(plane, (-shift) % WIDE, 1) if shift else plane
                value = value + weight * near[:, 128:128 + PW]
        return value

    def side_plane(n):
        low = 128 * (n + 1)
        first = jnp.where(y == 0, 0.0, halo[0, :, 128 * n:128 * (n + 1)].astype(F32))
        last = jnp.where(y == NY - 1, 0.0, halo[1, :, 128 * n:128 * (n + 1)].astype(F32))
        inner = [s_got[i, :, low:low + 128].astype(F32) for i in range(NC)]
        return jnp.concatenate([first] + inner + [last], axis=1)

    def order_cells(j):
        received(z_all.at[j, pl.ds(0, 3)], za_r.at[j])
        value = jnp.zeros((SRC, WIDE), F32)
        for q in range(NY):
            rows = slice((j * NY + q) * QUARTER, (j * NY + q + 1) * QUARTER)
            value = value + dot(z_all[j, q], perm[rows, :], NN)
        return value

    later_term = {}
    whole = y_full[3]
    for j in reversed(range(PANELS)):
        z_j = dot(whole, d_whole(j), NN).astype(BF16)
        z_own[j] = z_j
        if j > 0:
            term = dot(z_j, l_whole(j, j - 1), NN)
            if j - 1 in later_term:
                term = term + later_term[j - 1]
            share(7 - j, term)
        z_all[j, y] = z_j
        for d in (1, 2, 3):
            send(z_own.at[j], z_all.at[j, y], za_s.at[j], za_r.at[j], y_peer(d))
        if j > 0:
            for earlier in range(j - 1):
                more = dot(z_j, l_whole(j, earlier), NN)
                later_term[earlier] = later_term[earlier] + more if earlier in later_term else more
            if j == 3:
                received(halo, ha_r)
                field[...] = stencil(side_plane(0), -1) + stencil(side_plane(1), 1)
            else:
                grid[...] = order_cells(j + 1) if j == 2 else grid[...] + order_cells(j + 1)
            whole = (y_full[j - 1].astype(F32) - total(7 - j)).astype(BF16)

    z_f32 = [z_own[p].astype(F32) for p in range(PANELS)]
    for n in range(NC):
        block = jnp.zeros((SRC, 128), F32)
        for p in range(PANELS):
            piece = z_f32[p][:, (n // 4) * 128:(n // 4 + 1) * 128]
            piece = pltpu.roll(piece, ((p - n % 4) * PART) % 128, 1)
            block = jnp.where(lane // PART == p, piece, block)
        w_send[n] = block.astype(BF16)
    w_got[zc] = w_send[zc]
    for d in range(1, NC):
        send(w_send.at[c_index(d)], w_got.at[zc], wf_s, wf_r, c_peer(d))

    grid[...] = grid[...] + order_cells(1)
    field_all = field[...] + stencil(grid[...] + order_cells(0), 0)
    for n in range(NC):
        here = s_got[n, :, 0:128].astype(F32) * field_all[:, n * 128:(n + 1) * 128]
        g1_send[n] = jnp.sum(here, axis=0, keepdims=True)

    for d in range(1, NC):
        send(g1_send.at[c_index(d)], g1_got.at[d - 1], g1_s, g1_r, c_peer(d))
    received(g1_got, g1_r)
    group = g1_send[zc]
    for d in range(1, NC):
        group = group + g1_got[d - 1]
    g2_send[...] = group
    for d in range(1, 16):
        send(g2_send, g2_got.at[d - 1], g2_s, g2_r, s_peer(d))

    received(w_got.at[pl.ds(0, NC - 1)], wf_r)
    back = w_got[...].astype(F32).reshape(256, 128).T
    wave_out[...] = back.reshape(PANELS, PART, 256).astype(BF16)

    for j in range(PANELS):
        sent(dcols.at[j, pl.ds(0, 3), 0], dy_s.at[j])
        sent(z_all.at[j, pl.ds(0, 3)], za_s.at[j])
    sent(x_got.at[pl.ds(0, NC - 1)], xa_s)
    sent(s_got.at[pl.ds(0, NC - 1)], sa_s)
    for n in range(len(ORDER)):
        sent(lrows.at[0, pl.ds(0, 7)], mo_s.at[n])
    for step in range(7):
        sent(part_got.at[step], st_s.at[step])
    sent(halo, ha_s)
    sent(w_got.at[pl.ds(0, NC - 1)], wf_s)
    sent(g1_got, g1_s)

    received(g2_got, g2_r)
    for d in range(1, 16):
        group = group + g2_got[d - 1]
    grad_out[...] = group * (1.0 / 64.0)
    sent(g2_got, g2_s)


def shards(rhs, lower_blocks, dinv, adjoint_field, side_field, stencil_coef, cell_row):
    dma = pltpu.SemaphoreType.DMA
    units = (len(ORDER),)
    wavefield, gradient = pl.pallas_call(
        kernel,
        out_shape=(
            jax.ShapeDtypeStruct((PANELS, PART, 256), BF16),
            jax.ShapeDtypeStruct((1, 128), F32),
        ),
        in_specs=[pl.BlockSpec(memory_space=pl.ANY)] * 7,
        out_specs=(pl.BlockSpec(memory_space=pltpu.VMEM),) * 2,
        scratch_shapes=[
            pltpu.VMEM((PANELS, PART, 256), BF16),
            pltpu.VMEM((128, 256), BF16),
            pltpu.VMEM((2, 128, 256), BF16),
            pltpu.VMEM((27, PW), F32),
            pltpu.VMEM((32, 128), jnp.int32),
            pltpu.VMEM((PANELS, NY, NC, PART, QUARTER), BF16),
            pltpu.VMEM((6, NC, PART, PW), BF16),
            pltpu.VMEM((256, 128), BF16),
            pltpu.VMEM((NC, SRC, 128), BF16),
            pltpu.VMEM((256, 384), BF16),
            pltpu.VMEM((NC, SRC, 384), BF16),
            pltpu.VMEM((2, SRC, 256), BF16),
            pltpu.VMEM((16, 128), jnp.int32),
            pltpu.VMEM((4096, WIDE), BF16),
            pltpu.VMEM((PANELS, SRC, QUARTER), F32),
            pltpu.VMEM((7, SRC, PW), BF16),
            pltpu.VMEM((7, 3, SRC, PW), BF16),
            pltpu.VMEM((PANELS, SRC, PW), BF16),
            pltpu.VMEM((PANELS, SRC, QUARTER), BF16),
            pltpu.VMEM((PANELS, NY, SRC, QUARTER), BF16),
            pltpu.VMEM((SRC, WIDE), F32),
            pltpu.VMEM((SRC, PW), F32),
            pltpu.VMEM((NC, SRC, 128), BF16),
            pltpu.VMEM((NC, SRC, 128), BF16),
            pltpu.VMEM((NC, 1, 128), F32),
            pltpu.VMEM((NC - 1, 1, 128), F32),
            pltpu.VMEM((1, 128), F32),
            pltpu.VMEM((15, 1, 128), F32),
            dma((7,)),
            dma((PANELS,)), dma((PANELS,)),
            dma, dma,
            dma, dma,
            dma(units), dma(units), dma(units), dma(units), dma(units),
            dma((7,)), dma((7,)),
            dma((PANELS,)), dma((PANELS,)),
            dma, dma,
            dma, dma,
            dma, dma,
            dma, dma,
            pltpu.SemaphoreType.REGULAR((3,)),
        ],
        compiler_params=pltpu.CompilerParams(
            collective_id=0, has_side_effects=True, vmem_limit_bytes=64 * 1024 * 1024
        ),
        cost_estimate=pl.CostEstimate(flops=10**9, bytes_accessed=4 * 10**6, transcendentals=0),
    )(rhs, lower_blocks, dinv, adjoint_field, side_field, stencil_coef, cell_row.reshape(32, 128))
    return wavefield, gradient.reshape(128)


def solution(mesh):
    in_specs = (
        P(None, "tile", "src"),
        P(None, "tile", None),
        P(None, "tile", None),
        P("tile", "src"),
        P(None, "tile", "src"),
        P(),
        P(),
    )
    out_specs = (P(None, "tile", "src"), P("tile"))
    return jax.shard_map(shards, mesh=mesh, in_specs=in_specs, out_specs=out_specs, check_vma=False)
```

```python
import functools

import jax
import jax.numpy as jnp
from jax import lax
from jax.experimental import pallas as pl
from jax.experimental.pallas import tpu as pltpu
from jax.sharding import PartitionSpec as P

MESH = pl.DeviceIdType.MESH
F32 = jnp.float32
BF16 = jnp.bfloat16
NY = 4
NC = 8
PANELS = 4
PART = 32
HALF = 16
SRC = 32
QUARTER = 256
PW = 1024
WIDE = 1280
NN = (((1,), (0,)), ((), ()))
NT = (((1,), (1,)), ((), ()))

ORDER = [("d", 0), ("l", 0), ("d", 1), ("l", 1), ("l", 2), ("d", 2), ("l", 3), ("l", 4), ("l", 5), ("d", 3)]
QUARTERED = [(), (), (), (2,), (2,), (2,), (2,), (2,), (2,), (2,)]
SCHEDULE = {
    "start": [
        "push l0", "push d0", "spread d1", "spread d2", "spread d3", "push d1", "push l1",
    ],
    "first": [
        "pump d0", "push l2", "pump l0", "ready d0",
    ],
    0: [
        "pump d1", "push d2", "pump l1", "push l3", "finish d1", "push l4", "ready l0", "ready d1",
    ],
    1: [
        "pump l2", "push l5", "finish l1", "pump d2", "push d3", "finish l2", "pump l3", "ready l1",
        "take l20", "finish d2", "pump l4", "ready l2", "ready d2",
    ],
    2: [
        "finish l3", "pump l5", "finish l4", "pump d3", "ready l3", "take l30", "ready l4", "take l31",
        "finish l5", "finish d3", "ready l5", "ready d3",
    ],
}
PLACE = {unit: number for number, unit in enumerate(ORDER)}


def block_of(later, earlier):
    return later * (later - 1) // 2 + earlier


def dot(a, b, dims):
    return lax.dot_general(a, b, dims, preferred_element_type=F32)


def kernel(
    rhs, lower, dinv, adj, side, coef_all, cells_all,
    wave_out, grad_out,
    rhs_in, adj_in, side_in, coef, cells,
    dcols, lrows, x_send, x_got, s_send, s_got, halo, order, perm, acc,
    part_send, part_got, y_full, z_own, z_all, grid, field, w_send, w_got,
    g1_send, g1_got, g2_send, g2_got,
    in_s, dy_s, dy_r, xa_s, xa_r, sa_s, sa_r, mo_s, mz_r, mq_r, mx_r, mc_r, st_s, st_r,
    za_s, za_r, ha_s, ha_r, wf_s, wf_r, g1_s, g1_r, g2_s, g2_r, tick,
):
    s = lax.axis_index("src")
    t = lax.axis_index("tile")
    x, zh = lax.rem(s, 4), lax.div(s, 4)
    y, zc = lax.div(t, NC), lax.rem(t, NC)
    zl, core = lax.div(zc, 2), lax.rem(zc, 2)
    z = zh * 4 + zl

    def dev(x, y, z, c):
        return (lax.div(z, 4) * 4 + x, (y * 4 + lax.rem(z, 4)) * 2 + c)

    def y_peer(d):
        return dev(x, lax.rem(y + d, NY), z, core)

    def x_peer(d):
        return dev(lax.rem(x + d, 4), y, z, core)

    def z_peer(d):
        return dev(x, y, lax.rem(z + d + 16, 16), core)

    def c_index(d):
        return lax.rem(zc + d, NC)

    def c_peer(d):
        return (s, y * NC + c_index(d))

    def s_peer(d):
        return (lax.rem(s + d, 16), t)

    sibling = dev(x, y, z, 1 - core)

    def send(src, dst, send_sem, recv_sem, device):
        pltpu.make_async_remote_copy(
            src_ref=src, dst_ref=dst, send_sem=send_sem, recv_sem=recv_sem,
            device_id=device, device_id_type=MESH,
        ).start()

    def received(ref, sem):
        pltpu.make_async_remote_copy(
            src_ref=ref, dst_ref=ref, send_sem=sem, recv_sem=sem,
            device_id=sibling, device_id_type=MESH,
        ).wait_recv()

    def sent(ref, sem):
        pltpu.make_async_remote_copy(
            src_ref=ref, dst_ref=ref, send_sem=sem, recv_sem=sem,
            device_id=sibling, device_id_type=MESH,
        ).wait_send()

    def signal(sem, device):
        pl.semaphore_signal(sem, inc=1, device_id=device, device_id_type=MESH)

    barrier = pltpu.get_barrier_semaphore()
    peers = [y_peer(d) for d in (1, 2, 3)] + [c_peer(d) for d in range(1, NC)]
    peers += [z_peer(d) for d in (1, -1, 2, -2)] + [x_peer(d) for d in (1, 2, 3)]
    for peer in peers:
        signal(barrier, peer)

    own_cols = pl.ds(pl.multiple_of(y * QUARTER, QUARTER), QUARTER)
    own_rows = pl.ds(pl.multiple_of(zc * SRC, SRC), SRC)
    own_cells = pl.ds(pl.multiple_of(y * PW, PW), PW)
    loads = [
        pltpu.make_async_copy(rhs, rhs_in, in_s.at[0]),
        pltpu.make_async_copy(dinv.at[:, :, own_cols], dcols.at[:, y, zc], in_s.at[1]),
        pltpu.make_async_copy(lower, lrows.at[:, zc], in_s.at[2]),
        pltpu.make_async_copy(cells_all, cells, in_s.at[3]),
        pltpu.make_async_copy(adj, adj_in, in_s.at[4]),
        pltpu.make_async_copy(side, side_in, in_s.at[5]),
        pltpu.make_async_copy(coef_all.at[:, own_cells], coef, in_s.at[6]),
    ]
    for load in loads:
        load.start()
    loads[0].wait()
    x_send[...] = rhs_in[...].astype(F32).reshape(PANELS * PART, 256).T.astype(BF16)
    x_got[zc] = x_send[own_rows, :]
    loads[1].wait()
    loads[2].wait()
    pl.semaphore_wait(barrier, len(peers))

    def spread(j):
        for d in (1, 2, 3):
            cols = pl.ds(pl.multiple_of(lax.rem(y + d, NY) * QUARTER, QUARTER), QUARTER)
            send(dinv.at[j, :, cols], dcols.at[j, y, zc], dy_s.at[j], dy_r.at[j], y_peer(d))

    spread(0)
    for d in range(1, NC):
        part = pl.ds(pl.multiple_of(c_index(d) * SRC, SRC), SRC)
        send(x_send.at[part, :], x_got.at[zc], xa_s, xa_r, c_peer(d))

    def unit_ref(unit, slot):
        kind, number = unit
        return dcols.at[number, :, slot] if kind == "d" else lrows.at[number, slot]

    def unit_slots(unit, count):
        kind, number = unit
        return dcols.at[number, :, pl.ds(0, count)] if kind == "d" else lrows.at[number, pl.ds(0, count)]

    def quarter_ref(unit, slot):
        kind, number = unit
        if kind == "d":
            return dcols.at[number, x, slot]
        return lrows.at[number, slot, :, pl.ds(pl.multiple_of(x * QUARTER, QUARTER), QUARTER)]

    def quarters(count):
        rows, columns = {1: (1, 1), 2: (1, 2), 3: (3, 1), 6: (3, 2), 9: (3, 3)}[count]
        return dcols.at[0, pl.ds(0, rows), pl.ds(0, columns)]

    def slot_at(d):
        return lax.rem(zl + d, 4) * 2 + core

    from_slots = (3, 1, 2)

    def push(unit):
        n = PLACE[unit]
        if unit[0] == "d":
            received(dcols.at[unit[1], pl.ds(0, 3), 0], dy_r.at[unit[1]])
        far = 2 - 4 * lax.rem(core + n, 2)
        for k, d in enumerate((1, -1, far)):
            if k in QUARTERED[n]:
                ref, sem = quarter_ref(unit, zc), mq_r
            else:
                ref, sem = unit_ref(unit, zc), mz_r
            send(ref, ref, mo_s.at[n], sem.at[n], z_peer(d))
        mine = unit_ref(unit, zc)
        send(mine, mine, mo_s.at[n], mc_r.at[n], sibling)

    def to_sibling(unit, k):
        here = unit_ref(unit, slot_at(from_slots[k]))
        send(here, here, mo_s.at[PLACE[unit]], mc_r.at[PLACE[unit]], sibling)

    def pump(unit):
        n = PLACE[unit]
        if QUARTERED[n]:
            received(quarters(len(QUARTERED[n])), mq_r.at[n])
            for k in QUARTERED[n]:
                here = quarter_ref(unit, slot_at(from_slots[k]))
                for d in (1, 2, 3):
                    send(here, here, mo_s.at[n], mx_r.at[n], x_peer(d))
        direct = [k for k in range(3) if k not in QUARTERED[n]]
        if direct:
            received(unit_slots(unit, len(direct)), mz_r.at[n])
            for k in direct:
                to_sibling(unit, k)

    def finish(unit):
        n = PLACE[unit]
        if not QUARTERED[n]:
            return
        received(quarters(3 * len(QUARTERED[n])), mx_r.at[n])
        for k in QUARTERED[n]:
            to_sibling(unit, k)

    def ready(unit):
        received(unit_slots(unit, 4), mc_r.at[PLACE[unit]])

    def run(name):
        for step in SCHEDULE.get(name, ""):
            verb, what = step.split()
            kind, number = what[0], int(what[1:])
            if verb == "spread":
                spread(number)
            elif verb == "take":
                take(number // 10, number % 10)
            else:
                {"push": push, "pump": pump, "finish": finish, "ready": ready}[verb]((kind, number))

    def d_whole(j):
        return dcols[j].reshape(PW, QUARTER)

    def l_whole(later, earlier):
        return lrows[block_of(later, earlier)].reshape(QUARTER, PW)

    def take(later, earlier):
        acc[later] = acc[later] - dot(y_full[earlier], l_whole(later, earlier), NT)

    run("start")

    for d in (2, -2):
        signal(tick.at[0], z_peer(d))

    loads[4].wait()
    loads[5].wait()
    s_send[:, 0:128] = adj_in[...].astype(F32).T.astype(BF16)
    s_send[:, 128:256] = side_in[0].astype(F32).T.astype(BF16)
    s_send[:, 256:384] = side_in[1].astype(F32).T.astype(BF16)
    s_got[zc] = s_send[own_rows, :]

    loads[3].wait()
    order[0:8, :] = cells[pl.ds(pl.multiple_of(lax.rem(y + 3, NY) * 8, 8), 8), :]
    left = jnp.where(y == 0, -1, order[7:8, :])
    order[8:16, :] = cells[pl.ds(pl.multiple_of(lax.rem(y + 1, NY) * 8, 8), 8), :]
    right = jnp.where(y == NY - 1, -1, order[8:9, :])
    middle = cells[pl.ds(pl.multiple_of(y * 8, 8), 8), :]
    wanted = [left] + [middle[i:i + 1, :] for i in range(8)] + [right]

    def fill(i, carry):
        rows = lax.broadcasted_iota(jnp.int32, (QUARTER, 128), 0) + i * QUARTER
        at = pl.ds(pl.multiple_of(i * QUARTER, QUARTER), QUARTER)
        for n, row in enumerate(wanted):
            hit = jnp.where(rows == row, 1.0, 0.0).astype(BF16)
            perm[at, n * 128:(n + 1) * 128] = hit
        return carry

    lax.fori_loop(0, 16, fill, 0)

    lane = lax.broadcasted_iota(jnp.int32, (SRC, 128), 1)
    received(x_got.at[pl.ds(0, NC - 1)], xa_r)
    for p in range(PANELS):
        for half in range(2):
            block = jnp.zeros((SRC, 128), F32)
            for q in range(4):
                piece = pltpu.roll(x_got[half * 4 + q].astype(F32), ((q - p) * PART) % 128, 1)
                block = jnp.where(lane // PART == q, piece, block)
            acc[p, :, half * 128:(half + 1) * 128] = block

    def share(step, half, value):
        part_send[step, half] = value.astype(BF16)
        n = step * 2 + half
        for d in (1, 2, 3):
            send(part_send.at[step, half], part_got.at[step, half, d - 1], st_s.at[n], st_r.at[n], y_peer(d))

    def total(step, half):
        received(part_got.at[step, half], st_r.at[step * 2 + half])
        value = part_send[step, half].astype(F32)
        for d in range(3):
            value = value + part_got[step, half, d].astype(F32)
        return value

    halves = [slice(0, HALF), slice(HALF, SRC)]

    run("first")
    for j in range(PANELS):
        for half, some in enumerate(halves):
            if j > 0:
                y_full[j - 1, some, :] = total(j - 1, half).astype(BF16)
                acc[j, some, :] = acc[j, some, :] - dot(y_full[j - 1, some, :], l_whole(j, j - 1), NT)
            share(j, half, dot(acc[j, some, :].astype(BF16), d_whole(j), NT))
        run(j)
        if j == 0:
            pl.semaphore_wait(tick.at[0], 2)
            for d in (4, -4):
                signal(tick.at[1], z_peer(d))
        if j == 1:
            for d in range(1, NC):
                part = pl.ds(pl.multiple_of(c_index(d) * SRC, SRC), SRC)
                send(s_send.at[part, :], s_got.at[zc], sa_s, sa_r, c_peer(d))
            pl.semaphore_wait(tick.at[1], 2)
            for d in (1, 2, 3):
                signal(tick.at[2], x_peer(d))
        if j == 3:
            pl.semaphore_wait(tick.at[2], 3)
            received(s_got.at[pl.ds(0, NC - 1)], sa_r)
            send(s_got.at[7, :, pl.ds(128, 256)], halo.at[0], ha_s, ha_r, y_peer(1))
            send(s_got.at[0, :, pl.ds(128, 256)], halo.at[1], ha_s, ha_r, y_peer(3))

    loads[6].wait()
    zpos = lax.rem(lax.broadcasted_iota(jnp.int32, (1, PW), 1), 64)

    def stencil(plane, offset_x):
        value = jnp.zeros((SRC, PW), F32)
        for offset_y in (-1, 0, 1):
            for offset_z in (-1, 0, 1):
                number = (offset_x + 1) * 9 + (offset_y + 1) * 3 + (offset_z + 1)
                weight = coef[number:number + 1, :]
                if offset_z == -1:
                    weight = jnp.where(zpos > 0, weight, 0.0)
                if offset_z == 1:
                    weight = jnp.where(zpos < 63, weight, 0.0)
                shift = offset_y * 64 + offset_z
                near = pltpu.roll(plane, (-shift) % WIDE, 1) if shift else plane
                value = value + weight * near[:, 128:128 + PW]
        return value

    def side_plane(n):
        low = 128 * (n + 1)
        first = jnp.where(y == 0, 0.0, halo[0, :, 128 * n:128 * (n + 1)].astype(F32))
        last = jnp.where(y == NY - 1, 0.0, halo[1, :, 128 * n:128 * (n + 1)].astype(F32))
        inner = [s_got[i, :, low:low + 128].astype(F32) for i in range(NC)]
        return jnp.concatenate([first] + inner + [last], axis=1)

    def order_cells(j):
        received(z_all.at[j, pl.ds(0, 3)], za_r.at[j])
        value = jnp.zeros((SRC, WIDE), F32)
        for q in range(NY):
            rows = slice((j * NY + q) * QUARTER, (j * NY + q + 1) * QUARTER)
            value = value + dot(z_all[j, q], perm[rows, :], NN)
        return value

    later_term = {}
    for j in reversed(range(PANELS)):
        for half, some in enumerate(halves):
            if j == 3:
                whole = total(3, half).astype(BF16)
            else:
                whole = (y_full[j, some, :].astype(F32) - total(6 - j, half)).astype(BF16)
            z_some = dot(whole, d_whole(j), NN).astype(BF16)
            z_own[j, some, :] = z_some
            if j > 0:
                term = dot(z_some, l_whole(j, j - 1), NN)
                if j - 1 in later_term:
                    term = term + later_term[j - 1][some]
                share(7 - j, half, term)
        z_j = z_own[j]
        z_all[j, y] = z_j
        for d in (1, 2, 3):
            send(z_own.at[j], z_all.at[j, y], za_s.at[j], za_r.at[j], y_peer(d))
        if j > 0:
            for earlier in range(j - 1):
                more = dot(z_j, l_whole(j, earlier), NN)
                later_term[earlier] = later_term[earlier] + more if earlier in later_term else more
            if j == 3:
                received(halo, ha_r)
                field[...] = stencil(side_plane(0), -1) + stencil(side_plane(1), 1)
            else:
                grid[...] = order_cells(j + 1) if j == 2 else grid[...] + order_cells(j + 1)

    z_f32 = [z_own[p].astype(F32) for p in range(PANELS)]
    for n in range(NC):
        block = jnp.zeros((SRC, 128), F32)
        for p in range(PANELS):
            piece = z_f32[p][:, (n // 4) * 128:(n // 4 + 1) * 128]
            piece = pltpu.roll(piece, ((p - n % 4) * PART) % 128, 1)
            block = jnp.where(lane // PART == p, piece, block)
        w_send[n] = block.astype(BF16)
    w_got[zc] = w_send[zc]
    for d in range(1, NC):
        send(w_send.at[c_index(d)], w_got.at[zc], wf_s, wf_r, c_peer(d))

    grid[...] = grid[...] + order_cells(1)
    field_all = field[...] + stencil(grid[...] + order_cells(0), 0)
    for n in range(NC):
        here = s_got[n, :, 0:128].astype(F32) * field_all[:, n * 128:(n + 1) * 128]
        g1_send[n] = jnp.sum(here, axis=0, keepdims=True)

    for d in range(1, NC):
        send(g1_send.at[c_index(d)], g1_got.at[d - 1], g1_s, g1_r, c_peer(d))
    received(g1_got, g1_r)
    group = g1_send[zc]
    for d in range(1, NC):
        group = group + g1_got[d - 1]
    g2_send[...] = group
    for d in range(1, 16):
        send(g2_send, g2_got.at[d - 1], g2_s, g2_r, s_peer(d))

    received(w_got.at[pl.ds(0, NC - 1)], wf_r)
    back = w_got[...].astype(F32).reshape(256, 128).T
    wave_out[...] = back.reshape(PANELS, PART, 256).astype(BF16)

    for j in range(PANELS):
        sent(dcols.at[j, pl.ds(0, 3), 0], dy_s.at[j])
        sent(z_all.at[j, pl.ds(0, 3)], za_s.at[j])
    sent(x_got.at[pl.ds(0, NC - 1)], xa_s)
    sent(s_got.at[pl.ds(0, NC - 1)], sa_s)
    for n in range(len(ORDER)):
        sent(lrows.at[0, pl.ds(0, 7)], mo_s.at[n])
    for step in range(7):
        for half in range(2):
            sent(part_got.at[step, half], st_s.at[step * 2 + half])
    sent(halo, ha_s)
    sent(w_got.at[pl.ds(0, NC - 1)], wf_s)
    sent(g1_got, g1_s)

    received(g2_got, g2_r)
    for d in range(1, 16):
        group = group + g2_got[d - 1]
    grad_out[...] = group * (1.0 / 64.0)
    sent(g2_got, g2_s)


def shards(rhs, lower_blocks, dinv, adjoint_field, side_field, stencil_coef, cell_row):
    dma = pltpu.SemaphoreType.DMA
    units = (len(ORDER),)
    wavefield, gradient = pl.pallas_call(
        kernel,
        out_shape=(
            jax.ShapeDtypeStruct((PANELS, PART, 256), BF16),
            jax.ShapeDtypeStruct((1, 128), F32),
        ),
        in_specs=[pl.BlockSpec(memory_space=pl.ANY)] * 7,
        out_specs=(pl.BlockSpec(memory_space=pltpu.VMEM),) * 2,
        scratch_shapes=[
            pltpu.VMEM((PANELS, PART, 256), BF16),
            pltpu.VMEM((128, 256), BF16),
            pltpu.VMEM((2, 128, 256), BF16),
            pltpu.VMEM((27, PW), F32),
            pltpu.VMEM((32, 128), jnp.int32),
            pltpu.VMEM((PANELS, NY, NC, PART, QUARTER), BF16),
            pltpu.VMEM((6, NC, PART, PW), BF16),
            pltpu.VMEM((256, 128), BF16),
            pltpu.VMEM((NC, SRC, 128), BF16),
            pltpu.VMEM((256, 384), BF16),
            pltpu.VMEM((NC, SRC, 384), BF16),
            pltpu.VMEM((2, SRC, 256), BF16),
            pltpu.VMEM((16, 128), jnp.int32),
            pltpu.VMEM((4096, WIDE), BF16),
            pltpu.VMEM((PANELS, SRC, QUARTER), F32),
            pltpu.VMEM((7, 2, HALF, PW), BF16),
            pltpu.VMEM((7, 2, 3, HALF, PW), BF16),
            pltpu.VMEM((PANELS, SRC, PW), BF16),
            pltpu.VMEM((PANELS, SRC, QUARTER), BF16),
            pltpu.VMEM((PANELS, NY, SRC, QUARTER), BF16),
            pltpu.VMEM((SRC, WIDE), F32),
            pltpu.VMEM((SRC, PW), F32),
            pltpu.VMEM((NC, SRC, 128), BF16),
            pltpu.VMEM((NC, SRC, 128), BF16),
            pltpu.VMEM((NC, 1, 128), F32),
            pltpu.VMEM((NC - 1, 1, 128), F32),
            pltpu.VMEM((1, 128), F32),
            pltpu.VMEM((15, 1, 128), F32),
            dma((7,)),
            dma((PANELS,)), dma((PANELS,)),
            dma, dma,
            dma, dma,
            dma(units), dma(units), dma(units), dma(units), dma(units),
            dma((14,)), dma((14,)),
            dma((PANELS,)), dma((PANELS,)),
            dma, dma,
            dma, dma,
            dma, dma,
            dma, dma,
            pltpu.SemaphoreType.REGULAR((3,)),
        ],
        compiler_params=pltpu.CompilerParams(
            collective_id=0, has_side_effects=True, vmem_limit_bytes=64 * 1024 * 1024
        ),
        cost_estimate=pl.CostEstimate(flops=10**9, bytes_accessed=4 * 10**6, transcendentals=0),
    )(rhs, lower_blocks, dinv, adjoint_field, side_field, stencil_coef, cell_row.reshape(32, 128))
    return wavefield, gradient.reshape(128)


def solution(mesh):
    in_specs = (
        P(None, "tile", "src"),
        P(None, "tile", None),
        P(None, "tile", None),
        P("tile", "src"),
        P(None, "tile", "src"),
        P(),
        P(),
    )
    out_specs = (P(None, "tile", "src"), P("tile"))
    return jax.shard_map(shards, mesh=mesh, in_specs=in_specs, out_specs=out_specs, check_vma=False)
```

```python
import functools

import jax
import jax.numpy as jnp
from jax import lax
from jax.experimental import pallas as pl
from jax.experimental.pallas import tpu as pltpu
from jax.sharding import PartitionSpec as P

MESH = pl.DeviceIdType.MESH
F32 = jnp.float32
BF16 = jnp.bfloat16
NY = 4
NC = 8
PANELS = 4
PART = 32
HALF = 16
SRC = 32
QUARTER = 256
PW = 1024
WIDE = 1280
NN = (((1,), (0,)), ((), ()))
NT = (((1,), (1,)), ((), ()))

ORDER = [("d", 0), ("l", 0), ("d", 1), ("l", 1), ("l", 2), ("d", 2), ("l", 3), ("l", 4), ("l", 5), ("d", 3)]
QUARTERED = [(), (), (), (2,), (2,), (2,), (2,), (2,), (2,), (2,)]
SCHEDULE = {
    "start": [
        "push l0", "push d0", "spread d1", "spread d2", "spread d3", "push d1", "push l1",
    ],
    "first": [
        "pump d0", "push l2", "pump l0", "ready d0",
    ],
    0: [
        "pump d1", "push d2", "pump l1", "push l3", "finish d1", "push l4", "ready l0", "ready d1",
    ],
    1: [
        "pump l2", "push l5", "finish l1", "pump d2", "push d3", "finish l2", "pump l3", "ready l1",
        "take l20", "finish d2", "pump l4", "ready l2", "ready d2",
    ],
    2: [
        "finish l3", "pump l5", "finish l4", "pump d3", "ready l3", "take l30", "ready l4", "take l31",
        "finish l5", "finish d3", "ready l5", "ready d3",
    ],
}
PLACE = {unit: number for number, unit in enumerate(ORDER)}


def block_of(later, earlier):
    return later * (later - 1) // 2 + earlier


def dot(a, b, dims):
    return lax.dot_general(a, b, dims, preferred_element_type=F32)


def kernel(
    rhs, lower, dinv, adj, side, coef_all, cells_all,
    wave_out, grad_out,
    rhs_in, adj_in, side_in, coef, cells,
    dcols, lrows, x_send, x_got, s_send, s_got, halo, perm, acc,
    part_send, part_got, y_full, z_own, z_all, grid, field, w_send, w_got,
    g1_send, g1_got, g2_send, g2_got,
    in_s, dy_s, dy_r, xa_s, xa_r, sa_s, sa_r, mo_s, mz_r, mq_r, mx_r, mc_r, st_s, st_r,
    za_s, za_r, ha_s, ha_r, wf_s, wf_r, g1_s, g1_r, g2_s, g2_r, tick,
):
    s = lax.axis_index("src")
    t = lax.axis_index("tile")
    x, zh = lax.rem(s, 4), lax.div(s, 4)
    y, zc = lax.div(t, NC), lax.rem(t, NC)
    zl, core = lax.div(zc, 2), lax.rem(zc, 2)
    z = zh * 4 + zl

    def dev(x, y, z, c):
        return (lax.div(z, 4) * 4 + x, (y * 4 + lax.rem(z, 4)) * 2 + c)

    def y_peer(d):
        return dev(x, lax.rem(y + d, NY), z, core)

    def x_peer(d):
        return dev(lax.rem(x + d, 4), y, z, core)

    def z_peer(d):
        return dev(x, y, lax.rem(z + d + 16, 16), core)

    def c_index(d):
        return lax.rem(zc + d, NC)

    def c_peer(d):
        return (s, y * NC + c_index(d))

    def s_peer(d):
        return (lax.rem(s + d, 16), t)

    sibling = dev(x, y, z, 1 - core)

    def send(src, dst, send_sem, recv_sem, device):
        pltpu.make_async_remote_copy(
            src_ref=src, dst_ref=dst, send_sem=send_sem, recv_sem=recv_sem,
            device_id=device, device_id_type=MESH,
        ).start()

    def received(ref, sem):
        pltpu.make_async_remote_copy(
            src_ref=ref, dst_ref=ref, send_sem=sem, recv_sem=sem,
            device_id=sibling, device_id_type=MESH,
        ).wait_recv()

    def sent(ref, sem):
        pltpu.make_async_remote_copy(
            src_ref=ref, dst_ref=ref, send_sem=sem, recv_sem=sem,
            device_id=sibling, device_id_type=MESH,
        ).wait_send()

    def signal(sem, device):
        pl.semaphore_signal(sem, inc=1, device_id=device, device_id_type=MESH)

    barrier = pltpu.get_barrier_semaphore()
    peers = [y_peer(d) for d in (1, 2, 3)] + [c_peer(d) for d in range(1, NC)]
    peers += [z_peer(d) for d in (1, -1, 2, -2)] + [x_peer(d) for d in (1, 2, 3)]
    for peer in peers:
        signal(barrier, peer)

    own_cols = pl.ds(pl.multiple_of(y * QUARTER, QUARTER), QUARTER)
    own_rows = pl.ds(pl.multiple_of(zc * SRC, SRC), SRC)
    own_cells = pl.ds(pl.multiple_of(y * PW, PW), PW)
    loads = [
        pltpu.make_async_copy(rhs, rhs_in, in_s.at[0]),
        pltpu.make_async_copy(dinv.at[:, :, own_cols], dcols.at[:, y, zc], in_s.at[1]),
        pltpu.make_async_copy(lower, lrows.at[:, zc], in_s.at[2]),
        pltpu.make_async_copy(cells_all, cells, in_s.at[3]),
        pltpu.make_async_copy(adj, adj_in, in_s.at[4]),
        pltpu.make_async_copy(side, side_in, in_s.at[5]),
        pltpu.make_async_copy(coef_all.at[:, own_cells], coef, in_s.at[6]),
    ]
    for load in loads:
        load.start()
    loads[0].wait()
    x_send[...] = rhs_in[...].astype(F32).reshape(PANELS * PART, 256).T.astype(BF16)
    x_got[zc] = x_send[own_rows, :]
    loads[1].wait()
    loads[2].wait()
    pl.semaphore_wait(barrier, len(peers))

    def spread(j):
        for d in (2, 1, 3):
            cols = pl.ds(pl.multiple_of(lax.rem(y + d, NY) * QUARTER, QUARTER), QUARTER)
            send(dinv.at[j, :, cols], dcols.at[j, y, zc], dy_s.at[j], dy_r.at[j], y_peer(d))

    spread(0)
    for d in (4, 3, 5, 6, 2, 7, 1):
        part = pl.ds(pl.multiple_of(c_index(d) * SRC, SRC), SRC)
        send(x_send.at[part, :], x_got.at[zc], xa_s, xa_r, c_peer(d))

    def unit_ref(unit, slot):
        kind, number = unit
        return dcols.at[number, :, slot] if kind == "d" else lrows.at[number, slot]

    def unit_slots(unit, count):
        kind, number = unit
        return dcols.at[number, :, pl.ds(0, count)] if kind == "d" else lrows.at[number, pl.ds(0, count)]

    def quarter_ref(unit, slot):
        kind, number = unit
        if kind == "d":
            return dcols.at[number, x, slot]
        return lrows.at[number, slot, :, pl.ds(pl.multiple_of(x * QUARTER, QUARTER), QUARTER)]

    def quarters(count):
        rows, columns = {1: (1, 1), 2: (1, 2), 3: (3, 1), 6: (3, 2), 9: (3, 3)}[count]
        return dcols.at[0, pl.ds(0, rows), pl.ds(0, columns)]

    def slot_at(d):
        return lax.rem(zl + d, 4) * 2 + core

    from_slots = (3, 1, 2)

    def push(unit):
        n = PLACE[unit]
        if unit[0] == "d":
            received(dcols.at[unit[1], pl.ds(0, 3), 0], dy_r.at[unit[1]])
        far = 2 - 4 * lax.rem(core + n, 2)
        for k, d in ((2, far), (0, 1), (1, -1)):
            if k in QUARTERED[n]:
                ref, sem = quarter_ref(unit, zc), mq_r
            else:
                ref, sem = unit_ref(unit, zc), mz_r
            send(ref, ref, mo_s.at[n], sem.at[n], z_peer(d))
        mine = unit_ref(unit, zc)
        send(mine, mine, mo_s.at[n], mc_r.at[n], sibling)

    def to_sibling(unit, k):
        here = unit_ref(unit, slot_at(from_slots[k]))
        send(here, here, mo_s.at[PLACE[unit]], mc_r.at[PLACE[unit]], sibling)

    def pump(unit):
        n = PLACE[unit]
        if QUARTERED[n]:
            received(quarters(len(QUARTERED[n])), mq_r.at[n])
            for k in QUARTERED[n]:
                here = quarter_ref(unit, slot_at(from_slots[k]))
                for d in (2, 1, 3):
                    send(here, here, mo_s.at[n], mx_r.at[n], x_peer(d))
        direct = [k for k in range(3) if k not in QUARTERED[n]]
        if direct:
            received(unit_slots(unit, len(direct)), mz_r.at[n])
            for k in direct:
                to_sibling(unit, k)

    def finish(unit):
        n = PLACE[unit]
        if not QUARTERED[n]:
            return
        received(quarters(3 * len(QUARTERED[n])), mx_r.at[n])
        for k in QUARTERED[n]:
            to_sibling(unit, k)

    def ready(unit):
        received(unit_slots(unit, 4), mc_r.at[PLACE[unit]])

    def run(name):
        for step in SCHEDULE.get(name, ""):
            verb, what = step.split()
            kind, number = what[0], int(what[1:])
            if verb == "spread":
                spread(number)
            elif verb == "take":
                take(number // 10, number % 10)
            else:
                {"push": push, "pump": pump, "finish": finish, "ready": ready}[verb]((kind, number))

    def d_whole(j):
        return dcols[j].reshape(PW, QUARTER)

    def l_whole(later, earlier):
        return lrows[block_of(later, earlier)].reshape(QUARTER, PW)

    def take(later, earlier):
        acc[later] = acc[later] - dot(y_full[earlier], l_whole(later, earlier), NT)

    run("start")

    for d in (2, -2):
        signal(tick.at[0], z_peer(d))

    loads[4].wait()
    loads[5].wait()
    s_send[:, 0:128] = adj_in[...].astype(F32).T.astype(BF16)
    s_send[:, 128:256] = side_in[0].astype(F32).T.astype(BF16)
    s_send[:, 256:384] = side_in[1].astype(F32).T.astype(BF16)
    s_got[zc] = s_send[own_rows, :]

    loads[3].wait()
    def cells_from(number):
        return cells[pl.ds(pl.multiple_of(number * 128, 128), 128)].reshape(1, 128)

    left = jnp.where(y == 0, -1, cells_from(lax.rem(y + 3, NY) * 8 + 7))
    right = jnp.where(y == NY - 1, -1, cells_from(lax.rem(y + 1, NY) * 8))
    wanted = [left] + [cells_from(y * 8 + i) for i in range(8)] + [right]

    def fill(i, carry):
        rows = lax.broadcasted_iota(jnp.int32, (QUARTER, 128), 0) + i * QUARTER
        at = pl.ds(pl.multiple_of(i * QUARTER, QUARTER), QUARTER)
        for n, row in enumerate(wanted):
            hit = jnp.where(rows == row, 1.0, 0.0).astype(BF16)
            perm[at, n * 128:(n + 1) * 128] = hit
        return carry

    lax.fori_loop(0, 16, fill, 0)

    lane = lax.broadcasted_iota(jnp.int32, (SRC, 128), 1)
    received(x_got.at[pl.ds(0, NC - 1)], xa_r)
    for p in range(PANELS):
        for half in range(2):
            block = jnp.zeros((SRC, 128), F32)
            for q in range(4):
                piece = pltpu.roll(x_got[half * 4 + q].astype(F32), ((q - p) * PART) % 128, 1)
                block = jnp.where(lane // PART == q, piece, block)
            acc[p, :, half * 128:(half + 1) * 128] = block

    def share(step, half, value):
        part_send[step, half] = value.astype(BF16)
        n = step * 2 + half
        for d in (2, 1, 3):
            send(part_send.at[step, half], part_got.at[step, half, d - 1], st_s.at[n], st_r.at[n], y_peer(d))

    def total(step, half):
        received(part_got.at[step, half], st_r.at[step * 2 + half])
        value = part_send[step, half].astype(F32)
        for d in range(3):
            value = value + part_got[step, half, d].astype(F32)
        return value

    halves = [slice(0, HALF), slice(HALF, SRC)]

    run("first")
    for j in range(PANELS):
        for half, some in enumerate(halves):
            if j > 0:
                y_full[j - 1, some, :] = total(j - 1, half).astype(BF16)
                acc[j, some, :] = acc[j, some, :] - dot(y_full[j - 1, some, :], l_whole(j, j - 1), NT)
            share(j, half, dot(acc[j, some, :].astype(BF16), d_whole(j), NT))
        run(j)
        if j == 0:
            pl.semaphore_wait(tick.at[0], 2)
            for d in (4, -4):
                signal(tick.at[1], z_peer(d))
        if j == 1:
            for d in range(1, NC):
                part = pl.ds(pl.multiple_of(c_index(d) * SRC, SRC), SRC)
                send(s_send.at[part, :], s_got.at[zc], sa_s, sa_r, c_peer(d))
            pl.semaphore_wait(tick.at[1], 2)
            for d in (1, 2, 3):
                signal(tick.at[2], x_peer(d))
        if j == 3:
            pl.semaphore_wait(tick.at[2], 3)
            received(s_got.at[pl.ds(0, NC - 1)], sa_r)
            send(s_got.at[7, :, pl.ds(128, 256)], halo.at[0], ha_s, ha_r, y_peer(1))
            send(s_got.at[0, :, pl.ds(128, 256)], halo.at[1], ha_s, ha_r, y_peer(3))

    loads[6].wait()
    zpos = lax.rem(lax.broadcasted_iota(jnp.int32, (1, PW), 1), 64)

    def stencil(plane, offset_x):
        value = jnp.zeros((SRC, PW), F32)
        for offset_y in (-1, 0, 1):
            for offset_z in (-1, 0, 1):
                number = (offset_x + 1) * 9 + (offset_y + 1) * 3 + (offset_z + 1)
                weight = coef[number:number + 1, :]
                if offset_z == -1:
                    weight = jnp.where(zpos > 0, weight, 0.0)
                if offset_z == 1:
                    weight = jnp.where(zpos < 63, weight, 0.0)
                shift = offset_y * 64 + offset_z
                near = pltpu.roll(plane, (-shift) % WIDE, 1) if shift else plane
                value = value + weight * near[:, 128:128 + PW]
        return value

    def side_plane(n):
        low = 128 * (n + 1)
        first = jnp.where(y == 0, 0.0, halo[0, :, 128 * n:128 * (n + 1)].astype(F32))
        last = jnp.where(y == NY - 1, 0.0, halo[1, :, 128 * n:128 * (n + 1)].astype(F32))
        inner = [s_got[i, :, low:low + 128].astype(F32) for i in range(NC)]
        return jnp.concatenate([first] + inner + [last], axis=1)

    def order_cells(j):
        received(z_all.at[j, pl.ds(0, 3)], za_r.at[j])
        value = jnp.zeros((SRC, WIDE), F32)
        for q in range(NY):
            rows = slice((j * NY + q) * QUARTER, (j * NY + q + 1) * QUARTER)
            value = value + dot(z_all[j, q], perm[rows, :], NN)
        return value

    later_term = {}
    for j in reversed(range(PANELS)):
        for half, some in enumerate(halves):
            if j == 3:
                whole = total(3, half).astype(BF16)
            else:
                whole = (y_full[j, some, :].astype(F32) - total(6 - j, half)).astype(BF16)
            z_some = dot(whole, d_whole(j), NN).astype(BF16)
            z_own[j, some, :] = z_some
            if j > 0:
                term = dot(z_some, l_whole(j, j - 1), NN)
                if j - 1 in later_term:
                    term = term + later_term[j - 1][some]
                share(7 - j, half, term)
        z_j = z_own[j]
        z_all[j, y] = z_j
        for d in (2, 1, 3):
            send(z_own.at[j], z_all.at[j, y], za_s.at[j], za_r.at[j], y_peer(d))
        if j > 0:
            for earlier in range(j - 1):
                more = dot(z_j, l_whole(j, earlier), NN)
                later_term[earlier] = later_term[earlier] + more if earlier in later_term else more
            if j == 3:
                received(halo, ha_r)
                field[...] = stencil(side_plane(0), -1) + stencil(side_plane(1), 1)
            else:
                grid[...] = order_cells(j + 1) if j == 2 else grid[...] + order_cells(j + 1)

    z_f32 = [z_own[p].astype(F32) for p in range(PANELS)]
    for n in range(NC):
        block = jnp.zeros((SRC, 128), F32)
        for p in range(PANELS):
            piece = z_f32[p][:, (n // 4) * 128:(n // 4 + 1) * 128]
            piece = pltpu.roll(piece, ((p - n % 4) * PART) % 128, 1)
            block = jnp.where(lane // PART == p, piece, block)
        w_send[n] = block.astype(BF16)
    w_got[zc] = w_send[zc]
    for d in range(1, NC):
        send(w_send.at[c_index(d)], w_got.at[zc], wf_s, wf_r, c_peer(d))

    grid[...] = grid[...] + order_cells(1)
    field_all = field[...] + stencil(grid[...] + order_cells(0), 0)
    for n in range(NC):
        here = s_got[n, :, 0:128].astype(F32) * field_all[:, n * 128:(n + 1) * 128]
        g1_send[n] = jnp.sum(here, axis=0, keepdims=True)

    for d in (4, 3, 5, 6, 2, 7, 1):
        send(g1_send.at[c_index(d)], g1_got.at[d - 1], g1_s, g1_r, c_peer(d))
    received(w_got.at[pl.ds(0, NC - 1)], wf_r)
    back = w_got[...].astype(F32).reshape(256, 128).T
    wave_out[...] = back.reshape(PANELS, PART, 256).astype(BF16)

    for j in range(PANELS):
        sent(dcols.at[j, pl.ds(0, 3), 0], dy_s.at[j])
        sent(z_all.at[j, pl.ds(0, 3)], za_s.at[j])
    sent(x_got.at[pl.ds(0, NC - 1)], xa_s)
    sent(s_got.at[pl.ds(0, NC - 1)], sa_s)
    for n in range(len(ORDER)):
        sent(lrows.at[0, pl.ds(0, 7)], mo_s.at[n])
    for step in range(7):
        for half in range(2):
            sent(part_got.at[step, half], st_s.at[step * 2 + half])
    sent(halo, ha_s)
    sent(w_got.at[pl.ds(0, NC - 1)], wf_s)
    received(g1_got, g1_r)
    group = g1_send[zc]
    for d in range(1, NC):
        group = group + g1_got[d - 1]
    g2_send[...] = group
    for d in (8, 7, 9, 10, 6, 4, 12, 5, 11, 3, 13, 14, 2, 1, 15):
        send(g2_send, g2_got.at[d - 1], g2_s, g2_r, s_peer(d))

    sent(g1_got, g1_s)
    received(g2_got, g2_r)
    for d in range(1, 16):
        group = group + g2_got[d - 1]
    grad_out[...] = group * (1.0 / 64.0)
    sent(g2_got, g2_s)


def shards(rhs, lower_blocks, dinv, adjoint_field, side_field, stencil_coef, cell_row):
    dma = pltpu.SemaphoreType.DMA
    units = (len(ORDER),)
    wavefield, gradient = pl.pallas_call(
        kernel,
        out_shape=(
            jax.ShapeDtypeStruct((PANELS, PART, 256), BF16),
            jax.ShapeDtypeStruct((1, 128), F32),
        ),
        in_specs=[pl.BlockSpec(memory_space=pl.ANY)] * 7,
        out_specs=(pl.BlockSpec(memory_space=pltpu.VMEM),) * 2,
        scratch_shapes=[
            pltpu.VMEM((PANELS, PART, 256), BF16),
            pltpu.VMEM((128, 256), BF16),
            pltpu.VMEM((2, 128, 256), BF16),
            pltpu.VMEM((27, PW), F32),
            pltpu.VMEM((4096,), jnp.int32),
            pltpu.VMEM((PANELS, NY, NC, PART, QUARTER), BF16),
            pltpu.VMEM((6, NC, PART, PW), BF16),
            pltpu.VMEM((256, 128), BF16),
            pltpu.VMEM((NC, SRC, 128), BF16),
            pltpu.VMEM((256, 384), BF16),
            pltpu.VMEM((NC, SRC, 384), BF16),
            pltpu.VMEM((2, SRC, 256), BF16),
            pltpu.VMEM((4096, WIDE), BF16),
            pltpu.VMEM((PANELS, SRC, QUARTER), F32),
            pltpu.VMEM((7, 2, HALF, PW), BF16),
            pltpu.VMEM((7, 2, 3, HALF, PW), BF16),
            pltpu.VMEM((PANELS, SRC, PW), BF16),
            pltpu.VMEM((PANELS, SRC, QUARTER), BF16),
            pltpu.VMEM((PANELS, NY, SRC, QUARTER), BF16),
            pltpu.VMEM((SRC, WIDE), F32),
            pltpu.VMEM((SRC, PW), F32),
            pltpu.VMEM((NC, SRC, 128), BF16),
            pltpu.VMEM((NC, SRC, 128), BF16),
            pltpu.VMEM((NC, 1, 128), F32),
            pltpu.VMEM((NC - 1, 1, 128), F32),
            pltpu.VMEM((1, 128), F32),
            pltpu.VMEM((15, 1, 128), F32),
            dma((7,)),
            dma((PANELS,)), dma((PANELS,)),
            dma, dma,
            dma, dma,
            dma(units), dma(units), dma(units), dma(units), dma(units),
            dma((14,)), dma((14,)),
            dma((PANELS,)), dma((PANELS,)),
            dma, dma,
            dma, dma,
            dma, dma,
            dma, dma,
            pltpu.SemaphoreType.REGULAR((3,)),
        ],
        compiler_params=pltpu.CompilerParams(
            collective_id=0, has_side_effects=True, vmem_limit_bytes=64 * 1024 * 1024
        ),
        cost_estimate=pl.CostEstimate(flops=10**9, bytes_accessed=4 * 10**6, transcendentals=0),
    )(rhs, lower_blocks, dinv, adjoint_field, side_field, stencil_coef, cell_row)
    return wavefield, gradient.reshape(128)


def solution(mesh):
    in_specs = (
        P(None, "tile", "src"),
        P(None, "tile", None),
        P(None, "tile", None),
        P("tile", "src"),
        P(None, "tile", "src"),
        P(),
        P(),
    )
    out_specs = (P(None, "tile", "src"), P("tile"))
    return jax.shard_map(shards, mesh=mesh, in_specs=in_specs, out_specs=out_specs, check_vma=False)
```

```python
import functools

import jax
import jax.numpy as jnp
from jax import lax
from jax.experimental import pallas as pl
from jax.experimental.pallas import tpu as pltpu
from jax.sharding import PartitionSpec as P

MESH = pl.DeviceIdType.MESH
F32 = jnp.float32
BF16 = jnp.bfloat16
NY = 4
NC = 8
PANELS = 4
PART = 32
HALF = 16
SRC = 32
QUARTER = 256
PW = 1024
WIDE = 1280
NN = (((1,), (0,)), ((), ()))
NT = (((1,), (1,)), ((), ()))

ORDER = [("d", 0), ("l", 0), ("d", 1), ("l", 1), ("l", 2), ("d", 2), ("l", 3), ("l", 4), ("l", 5), ("d", 3)]
QUARTERED = [(), (), (), (2,), (2,), (2,), (2,), (2,), (2,), (2,)]
SCHEDULE = {
    "start": [
        "push l0", "push d0", "spread d1", "spread d2", "spread d3", "push d1", "push l1",
    ],
    "first": [
        "pump d0", "push l2", "pump l0", "ready d0",
    ],
    0: [
        "pump d1", "push d2", "pump l1", "push l3", "finish d1", "push l4", "ready l0", "ready d1",
    ],
    1: [
        "pump l2", "push l5", "finish l1", "pump d2", "push d3", "finish l2", "pump l3", "ready l1",
        "take l20", "finish d2", "pump l4", "ready l2", "ready d2",
    ],
    2: [
        "finish l3", "pump l5", "finish l4", "pump d3", "ready l3", "take l30", "ready l4", "take l31",
        "finish l5", "finish d3", "ready l5", "ready d3",
    ],
}
PLACE = {unit: number for number, unit in enumerate(ORDER)}


def block_of(later, earlier):
    return later * (later - 1) // 2 + earlier


def dot(a, b, dims):
    return lax.dot_general(a, b, dims, preferred_element_type=F32)


def kernel(
    rhs, lower, dinv, adj, side, coef_all, cells_all,
    wave_out, grad_out,
    rhs_in, adj_in, side_in, coef, cells,
    dcols, lrows, x_send, x_got, s_send, s_got, halo, perm, acc,
    part_send, part_got, y_full, z_own, z_all, grid, field, w_send, w_got,
    g1_send, g1_got, g2_send, g2_got,
    in_s, dy_s, dy_r, xa_s, xa_r, sa_s, sa_r, mo_s, mz_r, mq_r, mx_r, mc_r, st_s, st_r,
    za_s, za_r, ha_s, ha_r, wf_s, wf_r, g1_s, g1_r, g2_s, g2_r, tick,
):
    s = lax.axis_index("src")
    t = lax.axis_index("tile")
    x, zh = lax.rem(s, 4), lax.div(s, 4)
    y, zc = lax.div(t, NC), lax.rem(t, NC)
    zl, core = lax.div(zc, 2), lax.rem(zc, 2)
    z = zh * 4 + zl

    def dev(x, y, z, c):
        return (lax.div(z, 4) * 4 + x, (y * 4 + lax.rem(z, 4)) * 2 + c)

    def y_peer(d):
        return dev(x, lax.rem(y + d, NY), z, core)

    def x_peer(d):
        return dev(lax.rem(x + d, 4), y, z, core)

    def z_peer(d):
        return dev(x, y, lax.rem(z + d + 16, 16), core)

    def c_index(d):
        return lax.rem(zc + d, NC)

    def c_peer(d):
        return (s, y * NC + c_index(d))

    def s_peer(d):
        return (lax.rem(s + d, 16), t)

    sibling = dev(x, y, z, 1 - core)

    def send(src, dst, send_sem, recv_sem, device):
        pltpu.make_async_remote_copy(
            src_ref=src, dst_ref=dst, send_sem=send_sem, recv_sem=recv_sem,
            device_id=device, device_id_type=MESH,
        ).start()

    def received(ref, sem):
        pltpu.make_async_remote_copy(
            src_ref=ref, dst_ref=ref, send_sem=sem, recv_sem=sem,
            device_id=sibling, device_id_type=MESH,
        ).wait_recv()

    def sent(ref, sem):
        pltpu.make_async_remote_copy(
            src_ref=ref, dst_ref=ref, send_sem=sem, recv_sem=sem,
            device_id=sibling, device_id_type=MESH,
        ).wait_send()

    def signal(sem, device):
        pl.semaphore_signal(sem, inc=1, device_id=device, device_id_type=MESH)

    barrier = pltpu.get_barrier_semaphore()
    peers = [y_peer(d) for d in (1, 2, 3)] + [c_peer(d) for d in range(1, NC)]
    peers += [z_peer(d) for d in (1, -1, 2, -2)] + [x_peer(d) for d in (1, 2, 3)]
    for peer in peers:
        signal(barrier, peer)

    own_cols = pl.ds(pl.multiple_of(y * QUARTER, QUARTER), QUARTER)
    own_rows = pl.ds(pl.multiple_of(zc * SRC, SRC), SRC)
    own_cells = pl.ds(pl.multiple_of(y * PW, PW), PW)
    loads = [
        pltpu.make_async_copy(rhs, rhs_in, in_s.at[0]),
        pltpu.make_async_copy(dinv.at[:, :, own_cols], dcols.at[:, y, zc], in_s.at[1]),
        pltpu.make_async_copy(lower, lrows.at[:, zc], in_s.at[2]),
        pltpu.make_async_copy(cells_all, cells, in_s.at[3]),
        pltpu.make_async_copy(adj, adj_in, in_s.at[4]),
        pltpu.make_async_copy(side, side_in, in_s.at[5]),
        pltpu.make_async_copy(coef_all.at[:, own_cells], coef, in_s.at[6]),
    ]
    for load in loads:
        load.start()
    loads[0].wait()
    x_send[...] = rhs_in[...].astype(F32).reshape(PANELS * PART, 256).T.astype(BF16)
    x_got[zc] = x_send[own_rows, :]
    loads[1].wait()
    loads[2].wait()
    pl.semaphore_wait(barrier, len(peers))

    def spread(j):
        for d in (2, 1, 3):
            cols = pl.ds(pl.multiple_of(lax.rem(y + d, NY) * QUARTER, QUARTER), QUARTER)
            send(dinv.at[j, :, cols], dcols.at[j, y, zc], dy_s.at[j], dy_r.at[j], y_peer(d))

    spread(0)
    for d in (4, 3, 5, 6, 2, 7, 1):
        part = pl.ds(pl.multiple_of(c_index(d) * SRC, SRC), SRC)
        send(x_send.at[part, :], x_got.at[zc], xa_s, xa_r, c_peer(d))

    def unit_ref(unit, slot):
        kind, number = unit
        return dcols.at[number, :, slot] if kind == "d" else lrows.at[number, slot]

    def unit_slots(unit, count):
        kind, number = unit
        return dcols.at[number, :, pl.ds(0, count)] if kind == "d" else lrows.at[number, pl.ds(0, count)]

    def quarter_ref(unit, slot):
        kind, number = unit
        if kind == "d":
            return dcols.at[number, x, slot]
        return lrows.at[number, slot, :, pl.ds(pl.multiple_of(x * QUARTER, QUARTER), QUARTER)]

    def quarters(count):
        rows, columns = {1: (1, 1), 2: (1, 2), 3: (3, 1), 6: (3, 2), 9: (3, 3)}[count]
        return dcols.at[0, pl.ds(0, rows), pl.ds(0, columns)]

    def slot_at(d):
        return lax.rem(zl + d, 4) * 2 + core

    from_slots = (3, 1, 2)

    def push(unit):
        n = PLACE[unit]
        if unit[0] == "d":
            received(dcols.at[unit[1], pl.ds(0, 3), 0], dy_r.at[unit[1]])
        far = 2 - 4 * lax.rem(core + n, 2)
        for k, d in ((2, far), (0, 1), (1, -1)):
            if k in QUARTERED[n]:
                ref, sem = quarter_ref(unit, zc), mq_r
            else:
                ref, sem = unit_ref(unit, zc), mz_r
            send(ref, ref, mo_s.at[n], sem.at[n], z_peer(d))
        mine = unit_ref(unit, zc)
        send(mine, mine, mo_s.at[n], mc_r.at[n], sibling)

    def to_sibling(unit, k):
        here = unit_ref(unit, slot_at(from_slots[k]))
        send(here, here, mo_s.at[PLACE[unit]], mc_r.at[PLACE[unit]], sibling)

    def pump(unit):
        n = PLACE[unit]
        if QUARTERED[n]:
            received(quarters(len(QUARTERED[n])), mq_r.at[n])
            for k in QUARTERED[n]:
                here = quarter_ref(unit, slot_at(from_slots[k]))
                for d in (2, 1, 3):
                    send(here, here, mo_s.at[n], mx_r.at[n], x_peer(d))
        direct = [k for k in range(3) if k not in QUARTERED[n]]
        if direct:
            received(unit_slots(unit, len(direct)), mz_r.at[n])
            for k in direct:
                to_sibling(unit, k)

    def finish(unit):
        n = PLACE[unit]
        if not QUARTERED[n]:
            return
        received(quarters(3 * len(QUARTERED[n])), mx_r.at[n])
        for k in QUARTERED[n]:
            to_sibling(unit, k)

    def ready(unit):
        received(unit_slots(unit, 4), mc_r.at[PLACE[unit]])

    def run(name):
        for step in SCHEDULE.get(name, ""):
            verb, what = step.split()
            kind, number = what[0], int(what[1:])
            if verb == "spread":
                spread(number)
            elif verb == "take":
                take(number // 10, number % 10)
            else:
                {"push": push, "pump": pump, "finish": finish, "ready": ready}[verb]((kind, number))

    def d_whole(j):
        return dcols[j].reshape(PW, QUARTER)

    def l_whole(later, earlier):
        return lrows[block_of(later, earlier)].reshape(QUARTER, PW)

    def take(later, earlier):
        acc[later] = acc[later] - dot(y_full[earlier], l_whole(later, earlier), NT)

    run("start")

    for d in (2, -2):
        signal(tick.at[0], z_peer(d))

    loads[4].wait()
    loads[5].wait()
    s_send[:, 0:128] = adj_in[...].astype(F32).T.astype(BF16)
    s_send[:, 128:256] = side_in[0].astype(F32).T.astype(BF16)
    s_send[:, 256:384] = side_in[1].astype(F32).T.astype(BF16)
    s_got[zc] = s_send[own_rows, :]

    loads[3].wait()
    def cells_from(number):
        return cells[pl.ds(pl.multiple_of(number * 128, 128), 128)].reshape(1, 128)

    left = jnp.where(y == 0, -1, cells_from(lax.rem(y + 3, NY) * 8 + 7))
    right = jnp.where(y == NY - 1, -1, cells_from(lax.rem(y + 1, NY) * 8))
    wanted = [left] + [cells_from(y * 8 + i) for i in range(8)] + [right]

    def fill(i, carry):
        rows = lax.broadcasted_iota(jnp.int32, (QUARTER, 128), 0) + i * QUARTER
        at = pl.ds(pl.multiple_of(i * QUARTER, QUARTER), QUARTER)
        for n, row in enumerate(wanted):
            hit = jnp.where(rows == row, 1.0, 0.0).astype(BF16)
            perm[at, n * 128:(n + 1) * 128] = hit
        return carry

    lax.fori_loop(0, 16, fill, 0)

    lane = lax.broadcasted_iota(jnp.int32, (SRC, 128), 1)
    received(x_got.at[pl.ds(0, NC - 1)], xa_r)
    for p in range(PANELS):
        for half in range(2):
            block = jnp.zeros((SRC, 128), F32)
            for q in range(4):
                piece = pltpu.roll(x_got[half * 4 + q].astype(F32), ((q - p) * PART) % 128, 1)
                block = jnp.where(lane // PART == q, piece, block)
            acc[p, :, half * 128:(half + 1) * 128] = block

    def share(step, half, value):
        part_send[step, half] = value.astype(BF16)
        n = step * 2 + half
        for d in (2, 1, 3):
            send(part_send.at[step, half], part_got.at[step, half, d - 1], st_s.at[n], st_r.at[n], y_peer(d))

    def total(step, half):
        received(part_got.at[step, half], st_r.at[step * 2 + half])
        value = part_send[step, half].astype(F32)
        for d in range(3):
            value = value + part_got[step, half, d].astype(F32)
        return value

    halves = [slice(0, HALF), slice(HALF, SRC)]

    run("first")
    for j in range(PANELS):
        for half, some in enumerate(halves):
            if j > 0:
                y_full[j - 1, some, :] = total(j - 1, half).astype(BF16)
                acc[j, some, :] = acc[j, some, :] - dot(y_full[j - 1, some, :], l_whole(j, j - 1), NT)
            share(j, half, dot(acc[j, some, :].astype(BF16), d_whole(j), NT))
        run(j)
        if j == 0:
            pl.semaphore_wait(tick.at[0], 2)
            for d in (4, -4):
                signal(tick.at[1], z_peer(d))
        if j == 1:
            for d in (4, 3, 5, 6, 2, 7, 1):
                part = pl.ds(pl.multiple_of(c_index(d) * SRC, SRC), SRC)
                send(s_send.at[part, :], s_got.at[zc], sa_s, sa_r, c_peer(d))
            pl.semaphore_wait(tick.at[1], 2)
            for d in (1, 2, 3):
                signal(tick.at[2], x_peer(d))
        if j == 3:
            pl.semaphore_wait(tick.at[2], 3)
            received(s_got.at[pl.ds(0, NC - 1)], sa_r)
            send(s_got.at[7, :, pl.ds(128, 256)], halo.at[0], ha_s, ha_r, y_peer(1))
            send(s_got.at[0, :, pl.ds(128, 256)], halo.at[1], ha_s, ha_r, y_peer(3))

    loads[6].wait()
    zpos = lax.rem(lax.broadcasted_iota(jnp.int32, (1, PW), 1), 64)

    def stencil(plane, offset_x):
        value = jnp.zeros((SRC, PW), F32)
        for offset_y in (-1, 0, 1):
            for offset_z in (-1, 0, 1):
                number = (offset_x + 1) * 9 + (offset_y + 1) * 3 + (offset_z + 1)
                weight = coef[number:number + 1, :]
                if offset_z == -1:
                    weight = jnp.where(zpos > 0, weight, 0.0)
                if offset_z == 1:
                    weight = jnp.where(zpos < 63, weight, 0.0)
                shift = offset_y * 64 + offset_z
                near = pltpu.roll(plane, (-shift) % WIDE, 1) if shift else plane
                value = value + weight * near[:, 128:128 + PW]
        return value

    def side_plane(n):
        low = 128 * (n + 1)
        first = jnp.where(y == 0, 0.0, halo[0, :, 128 * n:128 * (n + 1)].astype(F32))
        last = jnp.where(y == NY - 1, 0.0, halo[1, :, 128 * n:128 * (n + 1)].astype(F32))
        inner = [s_got[i, :, low:low + 128].astype(F32) for i in range(NC)]
        return jnp.concatenate([first] + inner + [last], axis=1)

    def order_cells(j):
        received(z_all.at[j, pl.ds(0, 3)], za_r.at[j])
        value = jnp.zeros((SRC, WIDE), F32)
        for q in range(NY):
            rows = slice((j * NY + q) * QUARTER, (j * NY + q + 1) * QUARTER)
            value = value + dot(z_all[j, q], perm[rows, :], NN)
        return value

    later_term = {}
    for j in reversed(range(PANELS)):
        for half, some in enumerate(halves):
            if j == 3:
                whole = total(3, half).astype(BF16)
            else:
                whole = (y_full[j, some, :].astype(F32) - total(6 - j, half)).astype(BF16)
            z_some = dot(whole, d_whole(j), NN).astype(BF16)
            z_own[j, some, :] = z_some
            if j == 0:
                part = pl.ds(half * HALF, HALF)
                for d in (2, 1, 3):
                    send(z_own.at[0, part], z_all.at[0, y, part], za_s.at[0], za_r.at[0], y_peer(d))
            if j > 0:
                term = dot(z_some, l_whole(j, j - 1), NN)
                if j - 1 in later_term:
                    term = term + later_term[j - 1][some]
                share(7 - j, half, term)
        z_j = z_own[j]
        z_all[j, y] = z_j
        for d in (2, 1, 3) if j > 0 else ():
            send(z_own.at[j], z_all.at[j, y], za_s.at[j], za_r.at[j], y_peer(d))
        if j > 0:
            for earlier in range(j - 1):
                more = dot(z_j, l_whole(j, earlier), NN)
                later_term[earlier] = later_term[earlier] + more if earlier in later_term else more
            if j == 3:
                received(halo, ha_r)
                field[...] = stencil(side_plane(0), -1) + stencil(side_plane(1), 1)
            else:
                grid[...] = order_cells(j + 1) if j == 2 else grid[...] + order_cells(j + 1)

    z_f32 = [z_own[p].astype(F32) for p in range(PANELS)]
    for n in range(NC):
        block = jnp.zeros((SRC, 128), F32)
        for p in range(PANELS):
            piece = z_f32[p][:, (n // 4) * 128:(n // 4 + 1) * 128]
            piece = pltpu.roll(piece, ((p - n % 4) * PART) % 128, 1)
            block = jnp.where(lane // PART == p, piece, block)
        w_send[n] = block.astype(BF16)
    w_got[zc] = w_send[zc]
    for d in range(1, NC):
        send(w_send.at[c_index(d)], w_got.at[zc], wf_s, wf_r, c_peer(d))

    grid[...] = grid[...] + order_cells(1)
    field_all = field[...] + stencil(grid[...] + order_cells(0), 0)
    for n in range(NC):
        here = s_got[n, :, 0:128].astype(F32) * field_all[:, n * 128:(n + 1) * 128]
        g1_send[n] = jnp.sum(here, axis=0, keepdims=True)

    for d in (4, 3, 5, 6, 2, 7, 1):
        send(g1_send.at[c_index(d)], g1_got.at[d - 1], g1_s, g1_r, c_peer(d))
    received(w_got.at[pl.ds(0, NC - 1)], wf_r)
    back = w_got[...].astype(F32).reshape(256, 128).T
    wave_out[...] = back.reshape(PANELS, PART, 256).astype(BF16)

    for j in range(PANELS):
        sent(dcols.at[j, pl.ds(0, 3), 0], dy_s.at[j])
        sent(z_all.at[j, pl.ds(0, 3)], za_s.at[j])
    sent(x_got.at[pl.ds(0, NC - 1)], xa_s)
    sent(s_got.at[pl.ds(0, NC - 1)], sa_s)
    for n in range(len(ORDER)):
        sent(lrows.at[0, pl.ds(0, 7)], mo_s.at[n])
    for step in range(7):
        for half in range(2):
            sent(part_got.at[step, half], st_s.at[step * 2 + half])
    sent(halo, ha_s)
    sent(w_got.at[pl.ds(0, NC - 1)], wf_s)
    received(g1_got, g1_r)
    group = g1_send[zc]
    for d in range(1, NC):
        group = group + g1_got[d - 1]
    g2_send[...] = group
    for d in (8, 7, 9, 10, 6, 4, 12, 5, 11, 3, 13, 14, 2, 1, 15):
        send(g2_send, g2_got.at[d - 1], g2_s, g2_r, s_peer(d))

    sent(g1_got, g1_s)
    received(g2_got, g2_r)
    for d in range(1, 16):
        group = group + g2_got[d - 1]
    grad_out[...] = group * (1.0 / 64.0)
    sent(g2_got, g2_s)


def shards(rhs, lower_blocks, dinv, adjoint_field, side_field, stencil_coef, cell_row):
    dma = pltpu.SemaphoreType.DMA
    units = (len(ORDER),)
    wavefield, gradient = pl.pallas_call(
        kernel,
        out_shape=(
            jax.ShapeDtypeStruct((PANELS, PART, 256), BF16),
            jax.ShapeDtypeStruct((1, 128), F32),
        ),
        in_specs=[pl.BlockSpec(memory_space=pl.ANY)] * 7,
        out_specs=(pl.BlockSpec(memory_space=pltpu.VMEM),) * 2,
        scratch_shapes=[
            pltpu.VMEM((PANELS, PART, 256), BF16),
            pltpu.VMEM((128, 256), BF16),
            pltpu.VMEM((2, 128, 256), BF16),
            pltpu.VMEM((27, PW), F32),
            pltpu.VMEM((4096,), jnp.int32),
            pltpu.VMEM((PANELS, NY, NC, PART, QUARTER), BF16),
            pltpu.VMEM((6, NC, PART, PW), BF16),
            pltpu.VMEM((256, 128), BF16),
            pltpu.VMEM((NC, SRC, 128), BF16),
            pltpu.VMEM((256, 384), BF16),
            pltpu.VMEM((NC, SRC, 384), BF16),
            pltpu.VMEM((2, SRC, 256), BF16),
            pltpu.VMEM((4096, WIDE), BF16),
            pltpu.VMEM((PANELS, SRC, QUARTER), F32),
            pltpu.VMEM((7, 2, HALF, PW), BF16),
            pltpu.VMEM((7, 2, 3, HALF, PW), BF16),
            pltpu.VMEM((PANELS, SRC, PW), BF16),
            pltpu.VMEM((PANELS, SRC, QUARTER), BF16),
            pltpu.VMEM((PANELS, NY, SRC, QUARTER), BF16),
            pltpu.VMEM((SRC, WIDE), F32),
            pltpu.VMEM((SRC, PW), F32),
            pltpu.VMEM((NC, SRC, 128), BF16),
            pltpu.VMEM((NC, SRC, 128), BF16),
            pltpu.VMEM((NC, 1, 128), F32),
            pltpu.VMEM((NC - 1, 1, 128), F32),
            pltpu.VMEM((1, 128), F32),
            pltpu.VMEM((15, 1, 128), F32),
            dma((7,)),
            dma((PANELS,)), dma((PANELS,)),
            dma, dma,
            dma, dma,
            dma(units), dma(units), dma(units), dma(units), dma(units),
            dma((14,)), dma((14,)),
            dma((PANELS,)), dma((PANELS,)),
            dma, dma,
            dma, dma,
            dma, dma,
            dma, dma,
            pltpu.SemaphoreType.REGULAR((3,)),
        ],
        compiler_params=pltpu.CompilerParams(
            collective_id=0, has_side_effects=True, vmem_limit_bytes=64 * 1024 * 1024
        ),
        cost_estimate=pl.CostEstimate(flops=10**9, bytes_accessed=4 * 10**6, transcendentals=0),
    )(rhs, lower_blocks, dinv, adjoint_field, side_field, stencil_coef, cell_row)
    return wavefield, gradient.reshape(128)


def solution(mesh):
    in_specs = (
        P(None, "tile", "src"),
        P(None, "tile", None),
        P(None, "tile", None),
        P("tile", "src"),
        P(None, "tile", "src"),
        P(),
        P(),
    )
    out_specs = (P(None, "tile", "src"), P("tile"))
    return jax.shard_map(shards, mesh=mesh, in_specs=in_specs, out_specs=out_specs, check_vma=False)
```
